256 devices in a mesh: seq: 64 (over z, x, core), head: 4 (over y).
Axes of the slice: x: 4, y: 4, z: 8, core: 2. Of those that a mesh axis runs over, the one named last changes fastest.
Arguments:
- q_in: bfloat16 [8192, 2560], P('seq', 'head'), may hold values from -240 to 240
- k_in: bfloat16 [8192, 512], P('seq', 'head'), may hold values from -4 to 4
- v_in: bfloat16 [8192, 512], P('seq', 'head'), may hold values from -6 to 6
- x_in: bfloat16 [8192, 4096], P('seq', 'head'), may hold values from -400 to 400
- z_in: bfloat16 [8192, 4096], P('seq', 'head'), may hold values from -6 to 6
- b_in: bfloat16 [8192, 256], P('seq'), may hold values from -0.375 to 0.375
- c_in: bfloat16 [8192, 256], P('seq'), may hold values from -0.09375 to 0.09375
- dt_raw: float32 [8192, 64], P('seq', 'head'), may hold values from -4 to 4096
- a_log: float32 [64], P('head'), may hold values from -14 to -1.5
- d_skip: float32 [64], P('head'), may hold values from 0.5 to 1.5
- ssm_gain: float32 [4096], P('head'), may hold values from 0.5 to 1.5
- doc_start: int32 [8192], P('seq'), may hold values from 0 to 8191, as said below
Outputs:
- attn_out: bfloat16 [8192, 2560], P('seq', 'head')
- ssm_out: bfloat16 [8192, 4096], P('seq', 'head')
- attn_range: float32 [2, 2560], P(None, 'head')
- ssm_range: float32 [2, 4096], P(None, 'head')
The draws below stay inside these ranges and needn't reach their ends.
Inputs may be any that keep to these rules, and one draw needn't show every extreme that they name: doc_start[0] = 0; for every later position t, doc_start[t] is t or doc_start[t - 1].
All inputs are finite; a program needn't handle non-finite values.
Results may differ from the reference program's by a relative error of at most 0.0055.
Values may be sent and summed in bfloat16 or wider, within the bound.
No kernel may reach another device: no remote copies, remote signals or barrier semaphores. Data moves between devices by JAX's collectives and lax.ppermute only.
A program may use at most 256 MiB of HBM per device.

```python
import math
import jax
import jax.numpy as jnp
from jax import lax

TOK_DEV = 128
QH = 20
KVH = 4
HD = 128
SH = 64
HP = 64
NS = 256
WINDOW_TOKENS = 8192


def planted(key):
    key_query = jax.random.fold_in(key, 11)
    key_keys = jax.random.fold_in(key, 12)
    queries = 2.5 * jax.random.truncated_normal(key_query, -4.0, 4.0, (WINDOW_TOKENS, QH * HD), jnp.float32)
    key_rows = jax.random.truncated_normal(key_keys, -4.0, 4.0, (WINDOW_TOKENS, KVH * HD), jnp.float32)
    base_strength = 4.0
    unit_strength = 25.0 / math.sqrt(HD)
    period_len = min(509, max(WINDOW_TOKENS // 4, 61))
    positions = jnp.arange(WINDOW_TOKENS, dtype=jnp.int32)
    target = positions % period_len == period_len - 20
    second_value = positions % period_len == period_len - 56
    key_rows = jnp.where(second_value[:, None], 0.99 * jnp.roll(key_rows, 1, axis=0), key_rows)
    anchor = jnp.roll(key_rows, 37, axis=0).reshape(WINDOW_TOKENS, KVH, 1, HD)
    anchor = jnp.broadcast_to(anchor, (WINDOW_TOKENS, KVH, QH // KVH, HD)).reshape(WINDOW_TOKENS, QH * HD)
    level = (positions // period_len % 5).astype(jnp.float32)
    strength = (base_strength + level) * unit_strength
    queries = jnp.where(target[:, None], strength[:, None] * anchor, queries)
    return (queries, key_rows)


def draw_q_in(key, part):
    return planted(key)[0].astype(jnp.bfloat16)


def draw_k_in(key, part):
    return planted(key)[1].astype(jnp.bfloat16)


def draw_x_in(key, part):
    columns = (jnp.arange(SH * HP, dtype=jnp.int32) // HP).astype(jnp.float32)
    row_scale = jnp.exp(jax.random.uniform(jax.random.fold_in(key, 41), (WINDOW_TOKENS, 1), jnp.float32, 0.0, math.log(10.0)))
    noise = jax.random.truncated_normal(jax.random.fold_in(key, 42), -4.0, 4.0, (WINDOW_TOKENS, SH * HP), jnp.float32)
    column_scale = jnp.exp(math.log(10.0) * columns / max(SH - 1, 1))
    return (noise * row_scale * column_scale[None, :]).astype(jnp.bfloat16)


def draw_dt_raw(key, part):
    blocks_count = WINDOW_TOKENS // TOK_DEV
    offset = jax.random.uniform(jax.random.fold_in(key, 21), (blocks_count, 1, 1), jnp.float32, -1.0, 1.0)
    noise = 0.5 * jax.random.truncated_normal(jax.random.fold_in(key, 23), -4.0, 4.0, (blocks_count, TOK_DEV, SH), jnp.float32)
    initial_values = (noise + offset).reshape(WINDOW_TOKENS, SH)
    sorted_order = jax.random.permutation(jax.random.fold_in(key, 22), WINDOW_TOKENS)
    sudden_spike = sorted_order < 2
    return jnp.where(sudden_spike[:, None], jnp.float32(WINDOW_TOKENS // 2), initial_values)


def draw_a_log(key, part):
    chooser = jax.random.uniform(jax.random.fold_in(key, 31), (SH,), jnp.float32)
    share = 0.5
    slow_low, slow_high = (0.5 / WINDOW_TOKENS, 1.15 / WINDOW_TOKENS)
    gradual_rate = jax.random.uniform(jax.random.fold_in(key, 32), (SH,), jnp.float32, math.log(slow_low), math.log(slow_high))
    fast_rate = jax.random.uniform(jax.random.fold_in(key, 33), (SH,), jnp.float32, math.log(0.02), math.log(0.2))
    return jnp.where(chooser < share, gradual_rate, fast_rate)


def draw_doc_start(key, part):
    positions = jnp.arange(WINDOW_TOKENS, dtype=jnp.int32)
    sorted_order = jax.random.permutation(jax.random.fold_in(key, 51), WINDOW_TOKENS)
    starts = (sorted_order < 3) | (positions == 0) | (positions == WINDOW_TOKENS - 1)
    return lax.cummax(jnp.where(starts, positions, 0), axis=0).astype(jnp.int32)


def shard_levels(own_key, dims, split, smallest, high):
    factor_of = 1.0
    for position, blocks in split:
        heights = jax.random.uniform(jax.random.fold_in(jax.random.fold_in(own_key, 6), position), (blocks,), jnp.float32, smallest / len(split), high / len(split))
        factor_of = factor_of * jnp.repeat(jnp.exp(heights), dims[position] // blocks).reshape((-1,) + (1,) * (len(dims) - 1 - position))
    return factor_of


def gaussian(stream_key, extent, scale, bound, split=(), kind=jnp.bfloat16):
    array = scale * jax.random.normal(stream_key, extent, jnp.float32)
    if split:
        array = array * shard_levels(stream_key, extent, split, -0.22, 0.18)
    return jnp.clip(array, -bound, bound).astype(kind)


def setup_inputs(seed: int = 0) -> dict:
    keys = jax.random.split(jax.random.key(seed), 13)
    return {
        "q_in": draw_q_in(jax.random.fold_in(keys[12], 71), 0),
        "k_in": draw_k_in(jax.random.fold_in(keys[12], 71), 0),
        "v_in": gaussian(keys[2], (WINDOW_TOKENS, KVH * HD), 1.0, 6.0, ((0, 64), (1, 4))),
        "x_in": draw_x_in(jax.random.fold_in(keys[12], 71), 0),
        "z_in": gaussian(keys[4], (WINDOW_TOKENS, SH * HP), 1.0, 6.0, ((0, 64), (1, 4))),
        "b_in": gaussian(keys[5], (WINDOW_TOKENS, NS), NS ** -0.5, 0.375, ((0, 64),)),
        "c_in": gaussian(keys[6], (WINDOW_TOKENS, NS), (16 * NS) ** -0.5, 0.09375, ((0, 64),)),
        "dt_raw": draw_dt_raw(jax.random.fold_in(keys[12], 71), 0),
        "a_log": draw_a_log(jax.random.fold_in(keys[12], 71), 0),
        "d_skip": jnp.clip(0.5 + 1.0 * jax.random.uniform(keys[9], (SH,), jnp.float32) ** shard_levels(keys[9], (SH,), ((0, 4),), -0.2, 0.2), 0.5, 1.5),
        "ssm_gain": jnp.clip(1.0 + 0.1 * jax.random.normal(keys[10], (SH * HP,), jnp.float32), 0.5, 1.5),
        "doc_start": draw_doc_start(jax.random.fold_in(keys[12], 71), 0),
    }


epsilon = 1e-05

def attention(q_in, k_in, v_in, doc_start):
    group_size = QH // KVH
    block_rows = math.gcd(1024, WINDOW_TOKENS)
    score_scale = HD ** (-0.5)
    positions = jnp.arange(WINDOW_TOKENS, dtype=jnp.int32)
    out_blocks = []
    for first_row in range(0, WINDOW_TOKENS, block_rows):
        last_row = first_row + block_rows
        q_pos = positions[first_row:last_row]
        q_doc = doc_start[first_row:last_row]
        key_pos = positions[:last_row]
        visible = (key_pos[None, :] <= q_pos[:, None]) & (key_pos[None, :] >= q_doc[:, None])
        head_parts = []
        for kv_head in range(KVH):
            queries = q_in[first_row:last_row, kv_head * group_size * HD:(kv_head + 1) * group_size * HD]
            queries = queries.astype(jnp.float32).reshape(block_rows, group_size, HD)
            key_rows = k_in[:last_row, kv_head * HD:(kv_head + 1) * HD].astype(jnp.float32)
            value_rows = v_in[:last_row, kv_head * HD:(kv_head + 1) * HD].astype(jnp.float32)
            scores = jnp.einsum('rgd,sd->grs', queries, key_rows) * score_scale
            scores = jnp.where(visible[None], scores, -jnp.inf)
            highest = lax.optimization_barrier(jnp.max(scores, axis=-1, keepdims=True))
            weights = jnp.exp(scores - highest)
            totals = lax.optimization_barrier(jnp.sum(weights, axis=-1))
            rounded = lax.optimization_barrier(weights.astype(jnp.bfloat16)).astype(jnp.float32)
            mixed = jnp.einsum('grs,sd->rgd', rounded, value_rows) / jnp.transpose(totals)[:, :, None]
            head_parts.append(mixed.reshape(block_rows, group_size * HD))
        out_blocks.append(jnp.concatenate(head_parts, axis=1).astype(jnp.bfloat16))
    return jnp.concatenate(out_blocks, axis=0)

def block_summands(x_blk, b_blk, c_blk, dt_blk, a_log, doc_blk, begin):
    tok_rows = x_blk.shape[0]
    head_count = dt_blk.shape[1]
    step_len = jax.nn.softplus(dt_blk)
    log_decay = -step_len * jnp.exp(a_log)[None, :]
    running = jnp.cumsum(log_decay, axis=0)
    offsets = jnp.arange(tok_rows, dtype=jnp.int32)
    same_doc = (offsets[None, :] <= offsets[:, None]) & (begin + offsets[None, :] >= doc_blk[:, None])
    spread = jnp.where(same_doc[:, :, None], running[:, None, :] - running[None, :, :], 0.0)
    decay = jnp.where(same_doc[:, :, None], jnp.exp(spread), 0.0)
    inner = jnp.dot(c_blk, b_blk.T, preferred_element_type=jnp.float32)
    mixing = inner[:, :, None] * decay * step_len[None, :, :]
    values = x_blk.astype(jnp.float32).reshape(tok_rows, head_count, -1)
    intra = jnp.einsum('ijh,jhp->ihp', mixing, values, precision=lax.Precision.HIGHEST)
    reach = jnp.where((begin + offsets >= doc_blk[tok_rows - 1])[:, None], jnp.exp(running[tok_rows - 1][None, :] - running) * step_len, 0.0)
    local_state = jnp.dot(b_blk.astype(jnp.float32).T, (values * reach[:, :, None]).reshape(tok_rows, -1), precision=lax.Precision.HIGHEST)
    through = jnp.where(doc_blk[tok_rows - 1] < begin, jnp.exp(running[tok_rows - 1]), 0.0)
    entering = jnp.where((doc_blk < begin)[:, None], jnp.exp(running), 0.0)
    return (values, intra, local_state, through, entering)

def mamba(x_in, z_in, b_in, c_in, dt_raw, a_log, d_skip, ssm_gain, doc_start):
    blocks_count = WINDOW_TOKENS // TOK_DEV

    def advance(state, inputs):
        x_blk, b_blk, c_blk, dt_blk, doc_blk, begin = inputs
        values, intra, local_state, through, entering = block_summands(x_blk, b_blk, c_blk, dt_blk, a_log, doc_blk, begin)
        carried = jnp.dot(c_blk.astype(jnp.float32), state, precision=lax.Precision.HIGHEST)
        carried = carried.reshape(TOK_DEV, SH, HP) * entering[:, :, None]
        mixed = intra + carried + d_skip[None, :, None] * values
        state = state * jnp.repeat(through, HP)[None, :] + local_state
        return (state, mixed.reshape(TOK_DEV, SH * HP))
    starts = jnp.arange(blocks_count, dtype=jnp.int32) * TOK_DEV
    inputs = (x_in.reshape(blocks_count, TOK_DEV, SH * HP), b_in.reshape(blocks_count, TOK_DEV, NS), c_in.reshape(blocks_count, TOK_DEV, NS), dt_raw.reshape(blocks_count, TOK_DEV, SH), doc_start.reshape(blocks_count, TOK_DEV), starts)
    _, mixed = lax.scan(advance, jnp.zeros((NS, SH * HP), jnp.float32), inputs)
    gated = mixed.reshape(WINDOW_TOKENS, SH * HP) * jax.nn.silu(z_in.astype(jnp.float32))
    squared_value = lax.optimization_barrier(jnp.mean(gated * gated, axis=1, keepdims=True))
    return (gated * lax.rsqrt(squared_value + epsilon) * ssm_gain[None, :]).astype(jnp.bfloat16)

def reference(q_in, k_in, v_in, x_in, z_in, b_in, c_in, dt_raw, a_log, d_skip, ssm_gain, doc_start):
    attn_out = attention(q_in, k_in, v_in, doc_start)
    ssm_out = mamba(x_in, z_in, b_in, c_in, dt_raw, a_log, d_skip, ssm_gain, doc_start)
    attn_wide = attn_out.astype(jnp.float32)
    ssm_wide = ssm_out.astype(jnp.float32)
    attn_range = jnp.stack([lax.optimization_barrier(jnp.min(attn_wide, axis=0)), lax.optimization_barrier(jnp.max(attn_wide, axis=0))])
    ssm_range = jnp.stack([lax.optimization_barrier(jnp.min(ssm_wide, axis=0)), lax.optimization_barrier(jnp.max(ssm_wide, axis=0))])
    return (attn_out, ssm_out, attn_range, ssm_range)
```

```python
import functools
import math

import jax
import jax.numpy as jnp
from jax import lax
from jax.experimental import pallas as pl
from jax.experimental.pallas import tpu as pltpu
from jax.sharding import PartitionSpec as P

TOK = 128
GROUP = 5
HD = 128
HEADS = 16
HP = 64
NS = 256
COLS = 1024
HALF = 512
HALF_HEADS = 8
ALL_COLS = 4096
CHIPS = 32
EPSILON = 1e-05
FLOOR = -1e30
SCORE_SCALE = math.log2(math.e) / math.sqrt(HD)
F32 = jnp.float32
BF16 = jnp.bfloat16
HIGH = lax.Precision.HIGHEST

VMEM = pl.BlockSpec(memory_space=pltpu.VMEM)
SMEM = pl.BlockSpec(memory_space=pltpu.SMEM)
ANY = pl.BlockSpec(memory_space=pl.ANY)


def mm(a, b, dims=((1,), (0,)), precision=None):
    return lax.dot_general(a, b, (dims, ((), ())), precision=precision, preferred_element_type=F32)


def split_mm(a, b, dims=((1,), (0,)), which=0):
    wide = (a, b)[which]
    top = wide.astype(BF16)
    rest = (wide - top.astype(F32)).astype(BF16)
    if which == 0:
        return mm(top, b, dims) + mm(rest, b, dims)
    return mm(a, top, dims) + mm(a, rest, dims)


def iota(shape, dim):
    return lax.broadcasted_iota(jnp.int32, shape, dim)


def spread_heads(first_head, width):
    return jnp.where(
        iota((HEADS, width), 0) == first_head + iota((HEADS, width), 1) // HP, 1.0, 0.0
    ).astype(F32)


def step_sizes(dt_ref, a_ref):
    raw = dt_ref[...]
    step_t = jnp.maximum(raw, 0.0) + jnp.log1p(jnp.exp(-jnp.abs(raw)))
    rows, cols = iota((TOK, TOK), 0), iota((TOK, TOK), 1)
    eye = jnp.where(rows == cols, 1.0, 0.0).astype(F32)
    rate = jnp.exp(jnp.transpose(jnp.broadcast_to(a_ref[...], (TOK, HEADS))))
    upper = jnp.where(rows <= cols, 1.0, 0.0).astype(F32)
    running_t = mm(-step_t * rate, upper, precision=HIGH)
    both = mm(eye, jnp.concatenate([step_t, running_t], axis=0), ((1,), (1,)), precision=HIGH)
    return step_t, running_t, both[:, :HEADS], both[:, HEADS : 2 * HEADS]


def position(doc_smem):
    return lax.axis_index("seq"), doc_smem[0, 0], doc_smem[0, TOK - 1]


def local_kernel(scal, x_ref, b_ref, dt_ref, a_ref, keep_ref, send_ref):
    me, _, last_doc = position(scal)
    begin = me * TOK
    core = me % 2
    _, _, step_len, running = step_sizes(dt_ref, a_ref)
    last = running[TOK - 1 : TOK, :]
    live = begin + iota((TOK, HEADS), 0) >= last_doc
    reach = jnp.where(live, jnp.exp(last - running) * step_len, 0.0)
    through = jnp.where(last_doc < begin, jnp.exp(last), 0.0)
    stacked = jnp.concatenate([reach, jnp.broadcast_to(through, (8, HEADS))], axis=0)
    for half, out in ((core, keep_ref), (1 - core, send_ref)):
        wide = mm(stacked, spread_heads(half * HALF_HEADS, HALF), precision=HIGH)
        values = x_ref[:, pl.ds(pl.multiple_of(half * HALF, HALF), HALF)].astype(F32)
        out[0:NS, :] = split_mm(b_ref[...], values * wide[:TOK], ((0,), (0,)), which=1)
        out[NS : NS + 8, :] = wide[TOK:]


def intra_kernel(x_ref, b_ref, c_ref, dt_ref, a_ref, skip_ref, doc_ref, y_ref, enter_ref):
    begin = lax.axis_index("seq") * TOK
    step_t, running_t, _, running = step_sizes(dt_ref, a_ref)
    rows, cols = iota((TOK, TOK), 0), iota((TOK, TOK), 1)
    doc = jnp.transpose(jnp.broadcast_to(doc_ref[...], (TOK, TOK)).astype(F32)).astype(jnp.int32)
    same_doc = (cols <= rows) & (begin + cols >= doc)
    earlier = same_doc & (cols < rows)
    enter_ref[...] = jnp.where(doc[:, :HEADS] < begin, jnp.exp(running), 0.0)
    inner = jnp.where(same_doc, mm(c_ref[...], b_ref[...], ((1,), (1,))), 0.0)
    skip = mm(
        jnp.broadcast_to(skip_ref[...], (8, HEADS)), spread_heads(0, COLS), precision=HIGH
    )[0:1]
    left = iota((TOK, 2 * HP), 1) < HP
    for pair in range(HEADS // 2):
        parts = []
        for h in (2 * pair, 2 * pair + 1):
            gap = jnp.where(earlier, running[:, h : h + 1] - running_t[h : h + 1, :], 0.0)
            parts.append(inner * jnp.exp(gap) * step_t[h : h + 1, :])
        at = slice(pair * 2 * HP, (pair + 1) * 2 * HP)
        values = x_ref[:, at]
        both = split_mm(jnp.concatenate(parts, axis=0), values)
        y_ref[:, at] = jnp.where(left, both[:TOK], both[TOK:]) + skip[:, at] * values.astype(F32)


def chip_kernel(keep_ref, got_ref, out_ref):
    core = lax.axis_index("seq") % 2
    first = core == 0
    t_own, t_other = keep_ref[NS : NS + 1, :], got_ref[NS : NS + 1, :]
    f_own = jnp.where(first, t_other, 1.0)
    f_other = jnp.where(first, 1.0, t_own)
    through = t_own * t_other
    lines = [through[:, tile * 128 : tile * 128 + 128] for tile in range(4)]
    lines = jnp.concatenate(lines + [jnp.zeros((4, 128), F32)], axis=0)
    for chip in range(CHIPS):
        rows = slice(chip * 8, chip * 8 + 8)
        out_ref[chip, :, 0:HALF] = keep_ref[rows, :] * f_own + got_ref[rows, :] * f_other
        out_ref[chip, :, HALF : HALF + 128] = lines


def prefix_kernel(in_ref, out_ref):
    total = jnp.zeros((8, HALF), F32)
    for chip in range(CHIPS):
        out_ref[chip] = total
        if chip < CHIPS - 1:
            lines = in_ref[chip, :, HALF : HALF + 128]
            through = jnp.concatenate([lines[n : n + 1] for n in range(4)], axis=1)
            total = total * through + in_ref[chip, :, 0:HALF]


def enter_kernel(pre_ref, keep_ref, got_ref, mine_ref, send_ref):
    core = lax.axis_index("seq") % 2
    first = core == 0
    t_first = jnp.where(first, keep_ref[NS : NS + 1, :], got_ref[NS : NS + 1, :])
    for chip in range(CHIPS):
        rows = slice(chip * 8, chip * 8 + 8)
        before = pre_ref[chip]
        state = jnp.where(first, keep_ref[rows, :], got_ref[rows, :])
        after = before * t_first + state
        mine_ref[rows, :] = jnp.where(first, before, after)
        send_ref[rows, :] = jnp.where(first, after, before)


def mix_kernel(y_ref, enter_ref, c_ref, z_ref, mine_ref, got_ref, gated_ref, sq_ref):
    core = lax.axis_index("seq") % 2
    squares = jnp.zeros((TOK, 128), F32)
    for half, state in ((core, mine_ref), (1 - core, got_ref)):
        at = pl.ds(pl.multiple_of(half * HALF, HALF), HALF)
        wide = mm(enter_ref[...], spread_heads(half * HALF_HEADS, HALF), precision=HIGH)
        mixed = y_ref[:, at] + split_mm(c_ref[...], state[...], which=1) * wide
        gate = z_ref[:, at].astype(F32)
        gated = mixed * (gate / (1.0 + jnp.exp(-gate)))
        gated_ref[:, at] = gated
        power = gated * gated
        for tile in range(HALF // 128):
            squares += power[:, tile * 128 : tile * 128 + 128]
    ones = jnp.ones((8, 128), F32)
    sq_ref[...] = mm(ones, squares, ((1,), (1,)), precision=HIGH)


def finish_kernel(gated_ref, s0, s1, s2, s3, gain_ref, attn_rng, out_ref, rng_ref, lines):
    total = s0[...] + s1[...] + s2[...] + s3[...]
    scale = lax.rsqrt(total[0:1, :] / ALL_COLS + EPSILON)
    scale = jnp.transpose(jnp.broadcast_to(scale, (TOK, TOK)))
    lines[16:32, :] = attn_rng[...]
    for tile in range(COLS // 128):
        at = slice(tile * 128, tile * 128 + 128)
        out = (gated_ref[:, at] * scale * gain_ref[:, at]).astype(BF16)
        out_ref[:, at] = out
        wide = out.astype(F32)
        lines[tile : tile + 1, :] = jnp.min(wide, axis=0, keepdims=True)
        lines[8 + tile : 9 + tile, :] = jnp.min(-wide, axis=0, keepdims=True)
    packed = lines[...].astype(BF16)
    for dest in range(8):
        rng_ref[dest] = packed


def least_kernel(in_ref, out_ref):
    least = in_ref[0].astype(F32)
    for part in range(1, 8):
        least = jnp.minimum(least, in_ref[part].astype(F32))
    for dest in range(8):
        out_ref[dest] = least.astype(BF16)


def range_kernel(in_ref, attn_ref, ssm_ref):
    least = in_ref[0].astype(F32)
    for part in range(1, 8):
        least = jnp.minimum(least, in_ref[part].astype(F32))
    for tile in range(COLS // 128):
        at = slice(tile * 128, tile * 128 + 128)
        ssm_ref[0:1, at] = least[tile : tile + 1]
        ssm_ref[1:2, at] = -least[8 + tile : 9 + tile]
    for tile in range(GROUP):
        at = slice(tile * 128, tile * 128 + 128)
        attn_ref[0:1, at] = least[16 + tile : 17 + tile]
        attn_ref[1:2, at] = -least[21 + tile : 22 + tile]


def attn_kernel(scal, q_ref, doc_ref, *rest):
    parts, (out_ref, rng_ref, held, highest, totals, accum, sems) = rest[:8], rest[8:]
    copies = [
        pltpu.make_async_copy(part, held.at[n // 4, pl.ds((n % 4) * 8, 8)], sems.at[n])
        for n, part in enumerate(parts)
    ]
    for copy in copies:
        copy.start()
    me, first_doc, last_doc = position(scal)
    core, mine = me % 2, me // 2
    z_mine, x_mine = mine // 4, mine % 4
    doc = jnp.transpose(jnp.broadcast_to(doc_ref[...], (TOK, TOK)).astype(F32)).astype(jnp.int32)
    doc = jnp.concatenate([doc, doc], axis=1)
    q_pos = me * TOK + iota((TOK, 2 * TOK), 0)
    lane = iota((TOK, 2 * TOK), 1)
    key_lane = jnp.where(lane < TOK, core * TOK + lane, (1 - core) * TOK + lane - TOK)
    highest[...] = jnp.full(highest.shape, FLOOR, F32)
    totals[...] = jnp.zeros(totals.shape, F32)
    accum[...] = jnp.zeros(accum.shape, F32)
    for copy in copies:
        copy.wait()

    def absorb(chip, masked):
        flip = z_mine ^ (chip // 4)
        place = (flip % 2) * 4 + (flip // 2 % 2) * 2 + flip // 4
        slot = (x_mine ^ (chip % 4)) * 8 + place
        near, far = held[0, slot], held[1, slot]
        keys = jnp.concatenate([near[:, :HD], far[:, :HD]], axis=0)
        vals = jnp.concatenate([near[:, HD:], far[:, HD:]], axis=0)
        if masked:
            key_pos = chip * 2 * TOK + key_lane
            visible = (key_pos <= q_pos) & (key_pos >= doc)
        for g in range(GROUP):
            scores = mm(q_ref[:, g * HD : (g + 1) * HD], keys, ((1,), (1,)))
            if masked:
                scores = jnp.where(visible, scores, FLOOR)
            old = highest[g]
            new = jnp.maximum(old, jnp.max(scores, axis=1, keepdims=True))
            factor = jnp.exp2((old - new) * SCORE_SCALE)
            wide = jnp.concatenate([new, new], axis=1)
            weights = jnp.exp2((scores - wide) * SCORE_SCALE)
            if masked:
                weights = jnp.where(visible, weights, 0.0)
            highest[g] = new
            totals[g] = totals[g] * factor + (weights[:, :TOK] + weights[:, TOK:])
            accum[g] = accum[g] * factor + mm(weights.astype(BF16), vals)

    low = first_doc // (2 * TOK)
    middle = jnp.minimum((last_doc + 2 * TOK - 1) // (2 * TOK), mine)

    def edge(n, _):
        absorb(jnp.where(n == 0, mine, low + n - 1), True)
        return 0

    def inside(chip, _):
        absorb(chip, False)
        return 0

    lax.fori_loop(0, middle - low + 1, edge, 0)
    lax.fori_loop(middle, mine, inside, 0)
    rng_ref[...] = jnp.zeros(rng_ref.shape, F32)
    for g in range(GROUP):
        total = jnp.sum(totals[g], axis=1, keepdims=True)
        out = (accum[g] / total).astype(BF16)
        out_ref[:, g * HD : (g + 1) * HD] = out
        wide = out.astype(F32)
        rng_ref[g : g + 1, :] = jnp.min(wide, axis=0, keepdims=True)
        rng_ref[GROUP + g : GROUP + g + 1, :] = jnp.min(-wide, axis=0, keepdims=True)


def call(kernel, outs, specs, name, flops=0, data=0, exps=0, scratch=()):
    return pl.pallas_call(
        kernel,
        out_shape=[jax.ShapeDtypeStruct(shape, dtype) for shape, dtype in outs],
        in_specs=list(specs),
        out_specs=[VMEM] * len(outs),
        scratch_shapes=list(scratch),
        compiler_params=pltpu.CompilerParams(vmem_limit_bytes=40 * 2**20),
        cost_estimate=pl.CostEstimate(flops=flops, bytes_accessed=data, transcendentals=exps),
        name=name,
    )


def swap(value, bit):
    count = lax.axis_size("seq")
    return lax.ppermute(value, "seq", [(i, i ^ bit) for i in range(count)])


def body(q_in, k_in, v_in, x_in, z_in, b_in, c_in, dt_raw, a_log, d_skip, ssm_gain, doc_start):
    dt_t = dt_raw.T
    doc_row = doc_start[None, :]
    a_row, skip_row, gain_row = a_log[None, :], d_skip[None, :], ssm_gain[None, :]
    same_core = [[i for i in range(64) if i % 2 == core] for core in range(2)]
    plane = [[z * 8 + n for n in range(8)] for z in range(8)]
    column = [[z * 8 + n for z in range(8)] for n in range(8)]

    near = jnp.concatenate([k_in, v_in], axis=1)[None]
    for bit in (32, 16, 8):
        near = jnp.concatenate([near, swap(near, bit)], axis=0)
    own = [near] + [swap(near, bit) for bit in (2, 4, 6)]
    other = [swap(part, 1) for part in own]

    keep, send = call(
        local_kernel, [((NS + 8, HALF), F32)] * 2, [SMEM] + [VMEM] * 4, "local_state",
        flops=2 * 2 * TOK * NS * COLS, data=2**21,
    )(doc_row, x_in, b_in, dt_t, a_row)
    got = swap(send, 1)
    (chunks,) = call(
        chip_kernel, [((CHIPS, 8, HALF + 128), F32)], [VMEM] * 2, "chip_state", data=2**20
    )(keep, got)
    chunks = lax.all_to_all(chunks, "seq", 0, 0, tiled=True, axis_index_groups=same_core)
    (prefix,) = call(prefix_kernel, [((CHIPS, 8, HALF), F32)], [VMEM], "prefix", data=2**19)(chunks)
    prefix = lax.all_to_all(prefix, "seq", 0, 0, tiled=True, axis_index_groups=same_core)
    mine, theirs = call(
        enter_kernel, [((NS, HALF), F32)] * 2, [VMEM] * 3, "state_in", data=2**20
    )(prefix, keep, got)
    got_state = swap(theirs, 1)
    y_part, enter = call(
        intra_kernel, [((TOK, COLS), F32), ((TOK, HEADS), F32)], [VMEM] * 7, "intra",
        flops=4 * TOK * TOK * COLS * 2, data=2**20, exps=TOK * TOK * HEADS,
    )(x_in, b_in, c_in, dt_t, a_row, skip_row, doc_row)
    gated, square = call(
        mix_kernel, [((TOK, COLS), F32), ((8, TOK), F32)], [VMEM] * 6, "mix",
        flops=2 * TOK * NS * COLS, data=2**21,
    )(y_part, enter, c_in, z_in, mine, got_state)
    squares = [square] + [
        lax.ppermute(square, "head", [(i, i ^ bit) for i in range(4)]) for bit in (1, 2, 3)
    ]

    attn_out, attn_rng = call(
        attn_kernel, [((TOK, GROUP * HD), BF16), ((16, 128), F32)],
        [SMEM] + [VMEM] * 2 + [ANY] * 8, "attention",
        flops=4 * TOK * GROUP * HD * 8192, data=2**23, exps=TOK * GROUP * 8192,
        scratch=[
            pltpu.VMEM((2, CHIPS, TOK, 2 * HD), BF16),
            pltpu.VMEM((GROUP, TOK, HD), F32),
            pltpu.VMEM((GROUP, TOK, HD), F32),
            pltpu.VMEM((GROUP, TOK, HD), F32),
            pltpu.SemaphoreType.DMA((8,)),
        ],
    )(doc_row, q_in, doc_row, *own, *other)

    ssm_out, rng = call(
        finish_kernel, [((TOK, COLS), BF16), ((8, 32, 128), BF16)], [VMEM] * 7, "finish",
        data=2**20, scratch=[pltpu.VMEM((32, 128), F32)],
    )(gated, *squares, gain_row, attn_rng)
    rng = lax.all_to_all(rng, "seq", 0, 0, tiled=True, axis_index_groups=plane)
    (rng,) = call(least_kernel, [((8, 32, 128), BF16)], [VMEM], "least")(rng)
    rng = lax.all_to_all(rng, "seq", 0, 0, tiled=True, axis_index_groups=column)
    attn_range, ssm_range = call(
        range_kernel, [((2, GROUP * HD), F32), ((2, COLS), F32)], [VMEM], "ranges"
    )(rng)
    return (attn_out, ssm_out, attn_range, ssm_range)


def solution(mesh):
    return jax.shard_map(
        body,
        mesh=mesh,
        in_specs=(
            P("seq", "head"),
            P("seq", "head"),
            P("seq", "head"),
            P("seq", "head"),
            P("seq", "head"),
            P("seq", None),
            P("seq", None),
            P("seq", "head"),
            P("head"),
            P("head"),
            P("head"),
            P("seq"),
        ),
        out_specs=(P("seq", "head"), P("seq", "head"), P(None, "head"), P(None, "head")),
        check_vma=False,
    )
```

```python
import functools
import math

import jax
import jax.numpy as jnp
from jax import lax
from jax.experimental import pallas as pl
from jax.experimental.pallas import tpu as pltpu
from jax.sharding import PartitionSpec as P

TOK = 128
GROUP = 5
HD = 128
HEADS = 16
HP = 64
NS = 256
COLS = 1024
HALF = 512
HALF_HEADS = 8
ALL_COLS = 4096
CHIPS = 32
EPSILON = 1e-05
FLOOR = -1e30
SCORE_SCALE = math.log2(math.e) / math.sqrt(HD)
F32 = jnp.float32
BF16 = jnp.bfloat16
HIGH = lax.Precision.HIGHEST

VMEM = pl.BlockSpec(memory_space=pltpu.VMEM)
SMEM = pl.BlockSpec(memory_space=pltpu.SMEM)
ANY = pl.BlockSpec(memory_space=pl.ANY)


def mm(a, b, dims=((1,), (0,)), precision=None):
    return lax.dot_general(a, b, (dims, ((), ())), precision=precision, preferred_element_type=F32)


def split_mm(a, b, dims=((1,), (0,)), which=0):
    wide = (a, b)[which]
    top = wide.astype(BF16)
    rest = (wide - top.astype(F32)).astype(BF16)
    if which == 0:
        return mm(top, b, dims) + mm(rest, b, dims)
    return mm(a, top, dims) + mm(a, rest, dims)


def iota(shape, dim):
    return lax.broadcasted_iota(jnp.int32, shape, dim)


def spread_heads(first_head, width):
    return jnp.where(
        iota((HEADS, width), 0) == first_head + iota((HEADS, width), 1) // HP, 1.0, 0.0
    ).astype(F32)


def step_sizes(dt_ref, a_ref):
    raw = dt_ref[...]
    step_t = jnp.maximum(raw, 0.0) + jnp.log1p(jnp.exp(-jnp.abs(raw)))
    rows, cols = iota((TOK, TOK), 0), iota((TOK, TOK), 1)
    eye = jnp.where(rows == cols, 1.0, 0.0).astype(F32)
    rate = jnp.exp(jnp.transpose(jnp.broadcast_to(a_ref[...], (TOK, HEADS))))
    upper = jnp.where(rows <= cols, 1.0, 0.0).astype(F32)
    running_t = mm(-step_t * rate, upper, precision=HIGH)
    both = mm(eye, jnp.concatenate([step_t, running_t], axis=0), ((1,), (1,)), precision=HIGH)
    return step_t, running_t, both[:, :HEADS], both[:, HEADS : 2 * HEADS]


def position(doc_smem):
    return lax.axis_index("seq"), doc_smem[0, 0], doc_smem[0, TOK - 1]


def local_kernel(scal, x_ref, b_ref, dt_ref, a_ref, keep_ref, send_ref):
    me, _, last_doc = position(scal)
    begin = me * TOK
    core = me % 2
    _, _, step_len, running = step_sizes(dt_ref, a_ref)
    last = running[TOK - 1 : TOK, :]
    live = begin + iota((TOK, HEADS), 0) >= last_doc
    reach = jnp.where(live, jnp.exp(last - running) * step_len, 0.0)
    through = jnp.where(last_doc < begin, jnp.exp(last), 0.0)
    stacked = jnp.concatenate([reach, jnp.broadcast_to(through, (8, HEADS))], axis=0)
    for half, out in ((core, keep_ref), (1 - core, send_ref)):
        wide = mm(stacked, spread_heads(half * HALF_HEADS, HALF), precision=HIGH)
        values = x_ref[:, pl.ds(pl.multiple_of(half * HALF, HALF), HALF)].astype(F32)
        out[0:NS, :] = split_mm(b_ref[...], values * wide[:TOK], ((0,), (0,)), which=1)
        out[NS : NS + 8, :] = wide[TOK:]


def intra_kernel(x_ref, b_ref, c_ref, dt_ref, a_ref, skip_ref, doc_ref, y_ref, enter_ref):
    begin = lax.axis_index("seq") * TOK
    step_t, running_t, _, running = step_sizes(dt_ref, a_ref)
    rows, cols = iota((TOK, TOK), 0), iota((TOK, TOK), 1)
    doc = jnp.transpose(jnp.broadcast_to(doc_ref[...], (TOK, TOK)).astype(F32)).astype(jnp.int32)
    same_doc = (cols <= rows) & (begin + cols >= doc)
    earlier = same_doc & (cols < rows)
    enter_ref[...] = jnp.where(doc[:, :HEADS] < begin, jnp.exp(running), 0.0)
    inner = jnp.where(same_doc, mm(c_ref[...], b_ref[...], ((1,), (1,))), 0.0)
    skip = mm(
        jnp.broadcast_to(skip_ref[...], (8, HEADS)), spread_heads(0, COLS), precision=HIGH
    )[0:1]
    left = iota((TOK, 2 * HP), 1) < HP
    for pair in range(HEADS // 2):
        parts = []
        for h in (2 * pair, 2 * pair + 1):
            gap = jnp.where(earlier, running[:, h : h + 1] - running_t[h : h + 1, :], 0.0)
            parts.append(inner * jnp.exp(gap) * step_t[h : h + 1, :])
        at = slice(pair * 2 * HP, (pair + 1) * 2 * HP)
        values = x_ref[:, at]
        both = split_mm(jnp.concatenate(parts, axis=0), values)
        y_ref[:, at] = jnp.where(left, both[:TOK], both[TOK:]) + skip[:, at] * values.astype(F32)


def chip_kernel(keep_ref, got_ref, out_ref):
    core = lax.axis_index("seq") % 2
    first = core == 0
    t_own, t_other = keep_ref[NS : NS + 1, :], got_ref[NS : NS + 1, :]
    f_own = jnp.where(first, t_other, 1.0)
    f_other = jnp.where(first, 1.0, t_own)
    through = t_own * t_other
    lines = [through[:, tile * 128 : tile * 128 + 128] for tile in range(4)]
    lines = jnp.concatenate(lines + [jnp.zeros((4, 128), F32)], axis=0)
    for chip in range(CHIPS):
        rows = slice(chip * 8, chip * 8 + 8)
        out_ref[chip, :, 0:HALF] = keep_ref[rows, :] * f_own + got_ref[rows, :] * f_other
        out_ref[chip, :, HALF : HALF + 128] = lines


def prefix_kernel(in_ref, out_ref):
    total = jnp.zeros((8, HALF), F32)
    for chip in range(CHIPS):
        out_ref[chip] = total
        if chip < CHIPS - 1:
            lines = in_ref[chip, :, HALF : HALF + 128]
            through = jnp.concatenate([lines[n : n + 1] for n in range(4)], axis=1)
            total = total * through + in_ref[chip, :, 0:HALF]


def enter_kernel(pre_ref, keep_ref, got_ref, mine_ref, send_ref):
    core = lax.axis_index("seq") % 2
    first = core == 0
    t_first = jnp.where(first, keep_ref[NS : NS + 1, :], got_ref[NS : NS + 1, :])
    for chip in range(CHIPS):
        rows = slice(chip * 8, chip * 8 + 8)
        before = pre_ref[chip]
        state = jnp.where(first, keep_ref[rows, :], got_ref[rows, :])
        after = before * t_first + state
        mine_ref[rows, :] = jnp.where(first, before, after)
        send_ref[rows, :] = jnp.where(first, after, before)


def mix_kernel(y_ref, enter_ref, c_ref, z_ref, mine_ref, got_ref, gated_ref, sq_ref):
    core = lax.axis_index("seq") % 2
    squares = jnp.zeros((TOK, 128), F32)
    for half, state in ((core, mine_ref), (1 - core, got_ref)):
        at = pl.ds(pl.multiple_of(half * HALF, HALF), HALF)
        wide = mm(enter_ref[...], spread_heads(half * HALF_HEADS, HALF), precision=HIGH)
        mixed = y_ref[:, at] + split_mm(c_ref[...], state[...], which=1) * wide
        gate = z_ref[:, at].astype(F32)
        gated = mixed * (gate / (1.0 + jnp.exp(-gate)))
        gated_ref[:, at] = gated
        power = gated * gated
        for tile in range(HALF // 128):
            squares += power[:, tile * 128 : tile * 128 + 128]
    ones = jnp.ones((8, 128), F32)
    sq_ref[...] = mm(ones, squares, ((1,), (1,)), precision=HIGH)


def finish_kernel(gated_ref, s0, s1, s2, s3, gain_ref, attn_rng, out_ref, rng_ref, lines):
    total = s0[...] + s1[...] + s2[...] + s3[...]
    scale = lax.rsqrt(total[0:1, :] / ALL_COLS + EPSILON)
    scale = jnp.transpose(jnp.broadcast_to(scale, (TOK, TOK)))
    lines[16:32, :] = attn_rng[...]
    for tile in range(COLS // 128):
        at = slice(tile * 128, tile * 128 + 128)
        out = (gated_ref[:, at] * scale * gain_ref[:, at]).astype(BF16)
        out_ref[:, at] = out
        wide = out.astype(F32)
        lines[tile : tile + 1, :] = jnp.min(wide, axis=0, keepdims=True)
        lines[8 + tile : 9 + tile, :] = jnp.min(-wide, axis=0, keepdims=True)
    rng_ref[...] = lines[...].astype(BF16)


def least_kernel(own_ref, got_ref, out_ref):
    least = jnp.minimum(own_ref[...].astype(F32), got_ref[...].astype(F32)).astype(BF16)
    for dest in range(CHIPS):
        out_ref[dest] = least


def range_kernel(in_ref, attn_ref, ssm_ref):
    least = in_ref[0].astype(F32)
    for part in range(1, CHIPS):
        least = jnp.minimum(least, in_ref[part].astype(F32))
    for tile in range(COLS // 128):
        at = slice(tile * 128, tile * 128 + 128)
        ssm_ref[0:1, at] = least[tile : tile + 1]
        ssm_ref[1:2, at] = -least[8 + tile : 9 + tile]
    for tile in range(GROUP):
        at = slice(tile * 128, tile * 128 + 128)
        attn_ref[0:1, at] = least[16 + tile : 17 + tile]
        attn_ref[1:2, at] = -least[21 + tile : 22 + tile]


ROWS = GROUP * TOK


def attn_kernel(flips, span, first, final, doc_smem, q_ref, doc_ref, *rest):
    sides, rest = rest[: 4 * len(flips)], rest[4 * len(flips) :]
    if not first:
        (old_highest, old_totals, old_accum), rest = [rest[0].at[n] for n in range(3)], rest[1:]
    if final:
        out_ref, rng_ref, carry, q_rows = rest
    else:
        carry, q_rows = rest
    highest, totals, accum = [carry.at[n] for n in range(3)]
    me, first_doc, last_doc = position(doc_smem)
    core, z_mine, x_mine = me % 2, me // 8, me // 2 % 4
    wide = span * TOK
    width = 2 * len(flips) * wide
    lane = iota((TOK, wide), 1)
    lane = lane // TOK * (8 * TOK) + lane % TOK
    for g in range(GROUP):
        q_rows[g * TOK : (g + 1) * TOK, :] = q_ref[:, g * HD : (g + 1) * HD]

    def load(planes, which):
        refs = [sides[2 * n + which] for n in range(2 * len(flips))]
        at = [slice(0, HD) if ref.shape[2] == HD or which == 0 else slice(HD, 2 * HD) for ref in refs]
        return jnp.concatenate(
            [ref[planes, :, cols].reshape(wide, HD) for ref, cols in zip(refs, at)], axis=0
        )

    def hide(block, values):
        begins = [
            ((block * span * 4 + (x_mine ^ flip)) * 2 + side) * TOK
            for flip in flips
            for side in (core, 1 - core)
        ]
        key_pos = jnp.concatenate([begin + lane for begin in begins], axis=1)
        doc = jnp.transpose(jnp.broadcast_to(doc_ref[...], (TOK, TOK)).astype(F32))
        doc = jnp.concatenate([doc.astype(jnp.int32)] * (width // TOK), axis=1)
        q_pos = me * TOK + iota((TOK, width), 0)
        visible = (key_pos <= q_pos) & (key_pos >= doc)
        return jnp.where(jnp.concatenate([visible] * GROUP, axis=0), values, FLOOR)

    def score(block, masked):
        keys = load(pl.ds(block * span, span), 0)
        scores = mm(q_rows[...], keys, ((1,), (1,)))
        return hide(block, scores) if masked else scores

    def fold(join, values):
        total = values[:, :TOK]
        for n in range(1, width // TOK):
            total = join(total, values[:, n * TOK : (n + 1) * TOK])
        return total

    def find(block, masked):
        highest[...] = jnp.maximum(highest[...], fold(jnp.maximum, score(block, masked)))

    def add(block, masked):
        vals = load(pl.ds(block * span, span), 1)
        gap = score(block, masked) - jnp.concatenate([highest[...]] * (width // TOK), axis=1)
        weights = jnp.exp2(gap * SCORE_SCALE)
        totals[...] += fold(jnp.add, weights)
        accum[...] += mm(weights.astype(BF16), vals)

    size = span * 8 * TOK
    low, last = first_doc // size, z_mine // span
    inner = jnp.minimum((last_doc + size - 1) // size, last)

    def sweep(absorb):
        def edge(n, _):
            absorb(jnp.where(n == 0, last, low + n - 1), True)
            return 0

        def inside(block, _):
            absorb(block, False)
            return 0

        lax.fori_loop(0, inner - low + 1, edge, 0)
        lax.fori_loop(inner, last, inside, 0)

    highest[...] = jnp.full((ROWS, HD), FLOOR, F32) if first else old_highest[...]
    sweep(find)
    highest[...] = jnp.broadcast_to(jnp.max(highest[...], axis=1, keepdims=True), (ROWS, HD))
    if first:
        totals[...] = jnp.zeros((ROWS, HD), F32)
        accum[...] = jnp.zeros((ROWS, HD), F32)
    else:
        factor = jnp.exp2((old_highest[...] - highest[...]) * SCORE_SCALE)
        totals[...] = old_totals[...] * factor
        accum[...] = old_accum[...] * factor
    sweep(add)
    if not final:
        return
    rng_ref[...] = jnp.zeros(rng_ref.shape, F32)
    for g in range(GROUP):
        rows = slice(g * TOK, (g + 1) * TOK)
        total = jnp.sum(totals[rows, :], axis=1, keepdims=True)
        out = (accum[rows, :] / total).astype(BF16)
        out_ref[:, g * HD : (g + 1) * HD] = out
        values = out.astype(F32)
        rng_ref[g : g + 1, :] = jnp.min(values, axis=0, keepdims=True)
        rng_ref[GROUP + g : GROUP + g + 1, :] = jnp.min(-values, axis=0, keepdims=True)


def copies_kernel(k_ref, v_ref, out_ref):
    for dest in range(8):
        out_ref[dest, :, 0:HD] = k_ref[...]
        out_ref[dest, :, HD:] = v_ref[...]


ATTN_COST = 10**10


def call(kernel, outs, specs, name, scratch=(), flops=0):
    return pl.pallas_call(
        kernel,
        out_shape=[jax.ShapeDtypeStruct(shape, dtype) for shape, dtype in outs],
        in_specs=list(specs),
        out_specs=[VMEM] * len(outs),
        scratch_shapes=list(scratch),
        compiler_params=pltpu.CompilerParams(vmem_limit_bytes=40 * 2**20),
        cost_estimate=pl.CostEstimate(flops=flops, bytes_accessed=0, transcendentals=0),
        name=name,
    )


def swap(value, bit):
    count = lax.axis_size("seq")
    return lax.ppermute(value, "seq", [(i, i ^ bit) for i in range(count)])


def body(q_in, k_in, v_in, x_in, z_in, b_in, c_in, dt_raw, a_log, d_skip, ssm_gain, doc_start):
    dt_t = dt_raw.T
    doc_row = doc_start[None, :]
    a_row, skip_row, gain_row = a_log[None, :], d_skip[None, :], ssm_gain[None, :]
    same_core = [[i for i in range(64) if i % 2 == core] for core in range(2)]
    column = [[z * 8 + n for z in range(8)] for n in range(8)]

    (near,) = call(copies_kernel, [((8, TOK, 2 * HD), BF16)], [VMEM] * 2, "copies")(k_in, v_in)
    near = lax.all_to_all(near, "seq", 0, 0, tiled=True, axis_index_groups=column)

    def attend(parts, flips, span, first, final, carry, name):
        scratch = [pltpu.VMEM((ROWS, HD), BF16)]
        if final:
            outs = [((TOK, GROUP * HD), BF16), ((16, 128), F32)]
            scratch = [pltpu.VMEM((3, ROWS, HD), F32)] + scratch
        else:
            outs = [((3, ROWS, HD), F32)]
        refs = []
        for part in parts:
            other = [swap(value, 1) for value in part]
            refs += [part[0], part[-1], other[0], other[-1]]
        return call(
            functools.partial(attn_kernel, flips, span, first, final), outs,
            [SMEM] + [VMEM] * (2 + len(refs) + len(carry)), name, scratch=scratch, flops=ATTN_COST,
        )(doc_row, q_in, doc_row, *refs, *carry)

    keep, send = call(
        local_kernel, [((NS + 8, HALF), F32)] * 2, [SMEM] + [VMEM] * 4, "local_state"
    )(doc_row, x_in, b_in, dt_t, a_row)
    got = swap(send, 1)
    y_part, enter = call(
        intra_kernel, [((TOK, COLS), F32), ((TOK, HEADS), F32)], [VMEM] * 7, "intra"
    )(x_in, b_in, c_in, dt_t, a_row, skip_row, doc_row)
    (chunks,) = call(chip_kernel, [((CHIPS, 8, HALF + 128), F32)], [VMEM] * 2, "chip_state")(keep, got)
    chunks = lax.all_to_all(chunks, "seq", 0, 0, tiled=True, axis_index_groups=same_core)
    side1, side3 = swap(near, 2), swap(near, 6)
    carry = attend([[near]], (0,), 4, True, False, [], "attention_near")
    carry = attend([[side1], [side3]], (1, 3), 2, False, False, carry, "attention_sides")
    chunks, carry, y_part = lax.optimization_barrier((chunks, carry, y_part))
    far = [swap(side1[:, :, :HD], 6), swap(side3[:, :, HD:], 2)]
    (prefix,) = call(prefix_kernel, [((CHIPS, 8, HALF), F32)], [VMEM], "prefix")(chunks)
    prefix = lax.all_to_all(prefix, "seq", 0, 0, tiled=True, axis_index_groups=same_core)
    attn_out, attn_rng = attend([far], (2,), 4, False, True, carry, "attention_far")
    prefix, attn_rng = lax.optimization_barrier((prefix, attn_rng))
    mine, theirs = call(enter_kernel, [((NS, HALF), F32)] * 2, [VMEM] * 3, "state_in")(
        prefix, keep, got
    )
    got_state = swap(theirs, 1)
    gated, square = call(mix_kernel, [((TOK, COLS), F32), ((8, TOK), F32)], [VMEM] * 6, "mix")(
        y_part, enter, c_in, z_in, mine, got_state
    )
    squares = [square] + [
        lax.ppermute(square, "head", [(i, i ^ bit) for i in range(4)]) for bit in (1, 2, 3)
    ]

    ssm_out, rng = call(
        finish_kernel, [((TOK, COLS), BF16), ((32, 128), BF16)], [VMEM] * 7, "finish",
        scratch=[pltpu.VMEM((32, 128), F32)],
    )(gated, *squares, gain_row, attn_rng)
    (rng,) = call(least_kernel, [((CHIPS, 32, 128), BF16)], [VMEM] * 2, "least")(rng, swap(rng, 1))
    rng = lax.all_to_all(rng, "seq", 0, 0, tiled=True, axis_index_groups=same_core)
    attn_range, ssm_range = call(
        range_kernel, [((2, GROUP * HD), F32), ((2, COLS), F32)], [VMEM], "ranges"
    )(rng)
    return (attn_out, ssm_out, attn_range, ssm_range)


def solution(mesh):
    return jax.shard_map(
        body,
        mesh=mesh,
        in_specs=(
            P("seq", "head"),
            P("seq", "head"),
            P("seq", "head"),
            P("seq", "head"),
            P("seq", "head"),
            P("seq", None),
            P("seq", None),
            P("seq", "head"),
            P("head"),
            P("head"),
            P("head"),
            P("seq"),
        ),
        out_specs=(P("seq", "head"), P("seq", "head"), P(None, "head"), P(None, "head")),
        check_vma=False,
    )
```

```python
import functools
import math

import jax
import jax.numpy as jnp
from jax import lax
from jax.experimental import pallas as pl
from jax.experimental.pallas import tpu as pltpu
from jax.sharding import PartitionSpec as P

TOK = 128
GROUP = 5
HD = 128
HEADS = 16
HP = 64
NS = 256
COLS = 1024
HALF = 512
HALF_HEADS = 8
ALL_COLS = 4096
CHIPS = 32
EPSILON = 1e-05
FLOOR = -1e30
SCORE_SCALE = math.log2(math.e) / math.sqrt(HD)
F32 = jnp.float32
BF16 = jnp.bfloat16
HIGH = lax.Precision.HIGHEST

VMEM = pl.BlockSpec(memory_space=pltpu.VMEM)
SMEM = pl.BlockSpec(memory_space=pltpu.SMEM)
ANY = pl.BlockSpec(memory_space=pl.ANY)


def mm(a, b, dims=((1,), (0,)), precision=None):
    return lax.dot_general(a, b, (dims, ((), ())), precision=precision, preferred_element_type=F32)


def split_mm(a, b, dims=((1,), (0,)), which=0):
    wide = (a, b)[which]
    top = wide.astype(BF16)
    rest = (wide - top.astype(F32)).astype(BF16)
    if which == 0:
        return mm(top, b, dims) + mm(rest, b, dims)
    return mm(a, top, dims) + mm(a, rest, dims)


def iota(shape, dim):
    return lax.broadcasted_iota(jnp.int32, shape, dim)


def spread_heads(first_head, width):
    return jnp.where(
        iota((HEADS, width), 0) == first_head + iota((HEADS, width), 1) // HP, 1.0, 0.0
    ).astype(F32)


def step_sizes(dt_ref, a_ref):
    raw = dt_ref[...]
    step_t = jnp.maximum(raw, 0.0) + jnp.log1p(jnp.exp(-jnp.abs(raw)))
    rows, cols = iota((TOK, TOK), 0), iota((TOK, TOK), 1)
    eye = jnp.where(rows == cols, 1.0, 0.0).astype(F32)
    rate = jnp.exp(jnp.transpose(jnp.broadcast_to(a_ref[...], (TOK, HEADS))))
    upper = jnp.where(rows <= cols, 1.0, 0.0).astype(F32)
    running_t = mm(-step_t * rate, upper, precision=HIGH)
    both = mm(eye, jnp.concatenate([step_t, running_t], axis=0), ((1,), (1,)), precision=HIGH)
    return step_t, running_t, both[:, :HEADS], both[:, HEADS : 2 * HEADS]


def position(doc_smem):
    return lax.axis_index("seq"), doc_smem[0, 0], doc_smem[0, TOK - 1]


def local_kernel(scal, x_ref, b_ref, dt_ref, a_ref, keep_ref, send_ref):
    me, _, last_doc = position(scal)
    begin = me * TOK
    core = me % 2
    _, _, step_len, running = step_sizes(dt_ref, a_ref)
    last = running[TOK - 1 : TOK, :]
    live = begin + iota((TOK, HEADS), 0) >= last_doc
    reach = jnp.where(live, jnp.exp(last - running) * step_len, 0.0)
    through = jnp.where(last_doc < begin, jnp.exp(last), 0.0)
    stacked = jnp.concatenate([reach, jnp.broadcast_to(through, (8, HEADS))], axis=0)
    for half, out in ((core, keep_ref), (1 - core, send_ref)):
        wide = mm(stacked, spread_heads(half * HALF_HEADS, HALF), precision=HIGH)
        values = x_ref[:, pl.ds(pl.multiple_of(half * HALF, HALF), HALF)].astype(F32)
        out[0:NS, :] = split_mm(b_ref[...], values * wide[:TOK], ((0,), (0,)), which=1)
        out[NS : NS + 8, :] = wide[TOK:]


def intra_kernel(x_ref, b_ref, c_ref, dt_ref, a_ref, skip_ref, doc_ref, y_ref, enter_ref):
    begin = lax.axis_index("seq") * TOK
    step_t, running_t, _, running = step_sizes(dt_ref, a_ref)
    rows, cols = iota((TOK, TOK), 0), iota((TOK, TOK), 1)
    doc = jnp.transpose(jnp.broadcast_to(doc_ref[...], (TOK, TOK)).astype(F32)).astype(jnp.int32)
    same_doc = (cols <= rows) & (begin + cols >= doc)
    earlier = same_doc & (cols < rows)
    enter_ref[...] = jnp.where(doc[:, :HEADS] < begin, jnp.exp(running), 0.0)
    inner = jnp.where(same_doc, mm(c_ref[...], b_ref[...], ((1,), (1,))), 0.0)
    skip = mm(
        jnp.broadcast_to(skip_ref[...], (8, HEADS)), spread_heads(0, COLS), precision=HIGH
    )[0:1]
    left = iota((TOK, 2 * HP), 1) < HP
    for pair in range(HEADS // 2):
        parts = []
        for h in (2 * pair, 2 * pair + 1):
            gap = jnp.where(earlier, running[:, h : h + 1] - running_t[h : h + 1, :], 0.0)
            parts.append(inner * jnp.exp(gap) * step_t[h : h + 1, :])
        at = slice(pair * 2 * HP, (pair + 1) * 2 * HP)
        values = x_ref[:, at]
        both = split_mm(jnp.concatenate(parts, axis=0), values)
        y_ref[:, at] = jnp.where(left, both[:TOK], both[TOK:]) + skip[:, at] * values.astype(F32)


def chip_kernel(keep_ref, got_ref, out_ref):
    core = lax.axis_index("seq") % 2
    first = core == 0
    t_own, t_other = keep_ref[NS : NS + 1, :], got_ref[NS : NS + 1, :]
    f_own = jnp.where(first, t_other, 1.0)
    f_other = jnp.where(first, 1.0, t_own)
    through = t_own * t_other
    lines = [through[:, tile * 128 : tile * 128 + 128] for tile in range(4)]
    lines = jnp.concatenate(lines + [jnp.zeros((4, 128), F32)], axis=0)
    for chip in range(CHIPS):
        rows = slice(chip * 8, chip * 8 + 8)
        out_ref[chip, :, 0:HALF] = keep_ref[rows, :] * f_own + got_ref[rows, :] * f_other
        out_ref[chip, :, HALF : HALF + 128] = lines


def prefix_kernel(in_ref, out_ref):
    total = jnp.zeros((8, HALF), F32)
    for chip in range(CHIPS):
        out_ref[chip] = total
        if chip < CHIPS - 1:
            lines = in_ref[chip, :, HALF : HALF + 128]
            through = jnp.concatenate([lines[n : n + 1] for n in range(4)], axis=1)
            total = total * through + in_ref[chip, :, 0:HALF]


def enter_kernel(pre_ref, keep_ref, got_ref, mine_ref, send_ref):
    core = lax.axis_index("seq") % 2
    first = core == 0
    t_first = jnp.where(first, keep_ref[NS : NS + 1, :], got_ref[NS : NS + 1, :])
    for chip in range(CHIPS):
        rows = slice(chip * 8, chip * 8 + 8)
        before = pre_ref[chip]
        state = jnp.where(first, keep_ref[rows, :], got_ref[rows, :])
        after = before * t_first + state
        mine_ref[rows, :] = jnp.where(first, before, after)
        send_ref[rows, :] = jnp.where(first, after, before)


def mix_kernel(y_ref, enter_ref, c_ref, z_ref, mine_ref, got_ref, gated_ref, sq_ref):
    core = lax.axis_index("seq") % 2
    squares = jnp.zeros((TOK, 128), F32)
    for half, state in ((core, mine_ref), (1 - core, got_ref)):
        at = pl.ds(pl.multiple_of(half * HALF, HALF), HALF)
        wide = mm(enter_ref[...], spread_heads(half * HALF_HEADS, HALF), precision=HIGH)
        mixed = y_ref[:, at] + split_mm(c_ref[...], state[...], which=1) * wide
        gate = z_ref[:, at].astype(F32)
        gated = mixed * (gate / (1.0 + jnp.exp(-gate)))
        gated_ref[:, at] = gated
        power = gated * gated
        for tile in range(HALF // 128):
            squares += power[:, tile * 128 : tile * 128 + 128]
    ones = jnp.ones((8, 128), F32)
    sq_ref[...] = mm(ones, squares, ((1,), (1,)), precision=HIGH)


def finish_kernel(gated_ref, s0, s1, s2, s3, gain_ref, attn_rng, out_ref, rng_ref, lines):
    total = s0[...] + s1[...] + s2[...] + s3[...]
    scale = lax.rsqrt(total[0:1, :] / ALL_COLS + EPSILON)
    scale = jnp.transpose(jnp.broadcast_to(scale, (TOK, TOK)))
    lines[16:32, :] = attn_rng[...]
    for tile in range(COLS // 128):
        at = slice(tile * 128, tile * 128 + 128)
        out = (gated_ref[:, at] * scale * gain_ref[:, at]).astype(BF16)
        out_ref[:, at] = out
        wide = out.astype(F32)
        lines[tile : tile + 1, :] = jnp.min(wide, axis=0, keepdims=True)
        lines[8 + tile : 9 + tile, :] = jnp.min(-wide, axis=0, keepdims=True)
    rng_ref[...] = lines[...].astype(BF16)


def least_kernel(own_ref, got_ref, out_ref):
    least = jnp.minimum(own_ref[...].astype(F32), got_ref[...].astype(F32)).astype(BF16)
    for dest in range(CHIPS):
        out_ref[dest] = least


def range_kernel(in_ref, attn_ref, ssm_ref):
    least = in_ref[0].astype(F32)
    for part in range(1, CHIPS):
        least = jnp.minimum(least, in_ref[part].astype(F32))
    for tile in range(COLS // 128):
        at = slice(tile * 128, tile * 128 + 128)
        ssm_ref[0:1, at] = least[tile : tile + 1]
        ssm_ref[1:2, at] = -least[8 + tile : 9 + tile]
    for tile in range(GROUP):
        at = slice(tile * 128, tile * 128 + 128)
        attn_ref[0:1, at] = least[16 + tile : 17 + tile]
        attn_ref[1:2, at] = -least[21 + tile : 22 + tile]


ROWS = GROUP * TOK


def attn_kernel(flips, span, first, final, doc_smem, q_ref, doc_ref, *rest):
    sides, rest = rest[: 4 * len(flips)], rest[4 * len(flips) :]
    if not first:
        (old_highest, old_totals, old_accum), rest = [rest[0].at[n] for n in range(3)], rest[1:]
    if final:
        out_ref, rng_ref, carry, q_rows = rest
    else:
        carry, q_rows = rest
    highest, totals, accum = [carry.at[n] for n in range(3)]
    me, first_doc, last_doc = position(doc_smem)
    core, z_mine, x_mine = me % 2, me // 8, me // 2 % 4
    wide = span * TOK
    width = 2 * len(flips) * wide
    lane = iota((TOK, wide), 1)
    lane = lane // TOK * (8 * TOK) + lane % TOK
    for g in range(GROUP):
        q_rows[g * TOK : (g + 1) * TOK, :] = q_ref[:, g * HD : (g + 1) * HD]

    def load(planes, which):
        refs = [sides[2 * n + which] for n in range(2 * len(flips))]
        at = [slice(0, HD) if ref.shape[2] == HD or which == 0 else slice(HD, 2 * HD) for ref in refs]
        return jnp.concatenate(
            [ref[planes, :, cols].reshape(wide, HD) for ref, cols in zip(refs, at)], axis=0
        )

    def hide(block, values):
        begins = [
            ((block * span * 4 + (x_mine ^ flip)) * 2 + side) * TOK
            for flip in flips
            for side in (core, 1 - core)
        ]
        key_pos = jnp.concatenate([begin + lane for begin in begins], axis=1)
        doc = jnp.transpose(jnp.broadcast_to(doc_ref[...], (TOK, TOK)).astype(F32))
        doc = jnp.concatenate([doc.astype(jnp.int32)] * (width // TOK), axis=1)
        q_pos = me * TOK + iota((TOK, width), 0)
        visible = (key_pos <= q_pos) & (key_pos >= doc)
        return jnp.where(jnp.concatenate([visible] * GROUP, axis=0), values, FLOOR)

    def score(block, masked):
        keys = load(pl.ds(block * span, span), 0)
        scores = mm(q_rows[...], keys, ((1,), (1,)))
        return hide(block, scores) if masked else scores

    def fold(join, values):
        total = values[:, :TOK]
        for n in range(1, width // TOK):
            total = join(total, values[:, n * TOK : (n + 1) * TOK])
        return total

    def absorb(block, masked):
        vals = load(pl.ds(block * span, span), 1)
        scores = score(block, masked)
        old = highest[...]
        new = jnp.maximum(old, jnp.max(fold(jnp.maximum, scores), axis=1, keepdims=True))
        factor = jnp.exp2((old - new) * SCORE_SCALE)
        gap = scores - jnp.concatenate([new] * (width // TOK), axis=1)
        weights = jnp.exp2(gap * SCORE_SCALE)
        highest[...] = new
        totals[...] = totals[...] * factor + fold(jnp.add, weights)
        accum[...] = accum[...] * factor + mm(weights.astype(BF16), vals)

    size = span * 8 * TOK
    low, last = first_doc // size, z_mine // span
    inner = jnp.minimum((last_doc + size - 1) // size, last)

    def edge(n, _):
        absorb(jnp.where(n == 0, last, low + n - 1), True)
        return 0

    def inside(block, _):
        absorb(block, False)
        return 0

    if first:
        highest[...] = jnp.full((ROWS, HD), 0.1 * FLOOR, F32)
        totals[...] = jnp.zeros((ROWS, HD), F32)
        accum[...] = jnp.zeros((ROWS, HD), F32)
    else:
        highest[...] = old_highest[...]
        totals[...] = old_totals[...]
        accum[...] = old_accum[...]
    lax.fori_loop(0, inner - low + 1, edge, 0)
    lax.fori_loop(inner, last, inside, 0)
    if not final:
        return
    rng_ref[...] = jnp.zeros(rng_ref.shape, F32)
    for g in range(GROUP):
        rows = slice(g * TOK, (g + 1) * TOK)
        total = jnp.sum(totals[rows, :], axis=1, keepdims=True)
        out = (accum[rows, :] / total).astype(BF16)
        out_ref[:, g * HD : (g + 1) * HD] = out
        values = out.astype(F32)
        rng_ref[g : g + 1, :] = jnp.min(values, axis=0, keepdims=True)
        rng_ref[GROUP + g : GROUP + g + 1, :] = jnp.min(-values, axis=0, keepdims=True)


def copies_kernel(k_ref, v_ref, out_ref):
    for dest in range(8):
        out_ref[dest, :, 0:HD] = k_ref[...]
        out_ref[dest, :, HD:] = v_ref[...]


ATTN_COST = 10**10


def call(kernel, outs, specs, name, scratch=(), flops=0):
    return pl.pallas_call(
        kernel,
        out_shape=[jax.ShapeDtypeStruct(shape, dtype) for shape, dtype in outs],
        in_specs=list(specs),
        out_specs=[VMEM] * len(outs),
        scratch_shapes=list(scratch),
        compiler_params=pltpu.CompilerParams(vmem_limit_bytes=40 * 2**20),
        cost_estimate=pl.CostEstimate(flops=flops, bytes_accessed=0, transcendentals=0),
        name=name,
    )


def swap(value, bit):
    count = lax.axis_size("seq")
    return lax.ppermute(value, "seq", [(i, i ^ bit) for i in range(count)])


def body(q_in, k_in, v_in, x_in, z_in, b_in, c_in, dt_raw, a_log, d_skip, ssm_gain, doc_start):
    dt_t = dt_raw.T
    doc_row = doc_start[None, :]
    a_row, skip_row, gain_row = a_log[None, :], d_skip[None, :], ssm_gain[None, :]
    same_core = [[i for i in range(64) if i % 2 == core] for core in range(2)]
    column = [[z * 8 + n for z in range(8)] for n in range(8)]

    (near,) = call(copies_kernel, [((8, TOK, 2 * HD), BF16)], [VMEM] * 2, "copies")(k_in, v_in)
    near = lax.all_to_all(near, "seq", 0, 0, tiled=True, axis_index_groups=column)

    def attend(parts, flips, span, first, final, carry, name):
        scratch = [pltpu.VMEM((ROWS, HD), BF16)]
        if final:
            outs = [((TOK, GROUP * HD), BF16), ((16, 128), F32)]
            scratch = [pltpu.VMEM((3, ROWS, HD), F32)] + scratch
        else:
            outs = [((3, ROWS, HD), F32)]
        refs = []
        for part in parts:
            other = [swap(value, 1) for value in part]
            refs += [part[0], part[-1], other[0], other[-1]]
        return call(
            functools.partial(attn_kernel, flips, span, first, final), outs,
            [SMEM] + [VMEM] * (2 + len(refs) + len(carry)), name, scratch=scratch, flops=ATTN_COST,
        )(doc_row, q_in, doc_row, *refs, *carry)

    keep, send = call(
        local_kernel, [((NS + 8, HALF), F32)] * 2, [SMEM] + [VMEM] * 4, "local_state"
    )(doc_row, x_in, b_in, dt_t, a_row)
    got = swap(send, 1)
    y_part, enter = call(
        intra_kernel, [((TOK, COLS), F32), ((TOK, HEADS), F32)], [VMEM] * 7, "intra"
    )(x_in, b_in, c_in, dt_t, a_row, skip_row, doc_row)
    (chunks,) = call(chip_kernel, [((CHIPS, 8, HALF + 128), F32)], [VMEM] * 2, "chip_state")(keep, got)
    near, chunks, y_part = lax.optimization_barrier((near, chunks, y_part))
    chunks = lax.all_to_all(chunks, "seq", 0, 0, tiled=True, axis_index_groups=same_core)
    side1, side3 = swap(near, 2), swap(near, 6)
    carry = attend([[near]], (0,), 4, True, False, [], "attention_near")
    far = [swap(side1[:, :, :HD], 6), swap(side3[:, :, HD:], 2)]
    chunks, _, _ = lax.optimization_barrier((chunks, carry, far))
    carry = attend([[side1], [side3]], (1, 3), 2, False, False, carry, "attention_sides")
    (prefix,) = call(prefix_kernel, [((CHIPS, 8, HALF), F32)], [VMEM], "prefix")(chunks)
    prefix = lax.all_to_all(prefix, "seq", 0, 0, tiled=True, axis_index_groups=same_core)
    attn_out, attn_rng = attend([far], (2,), 4, False, True, carry, "attention_far")
    prefix, attn_rng = lax.optimization_barrier((prefix, attn_rng))
    mine, theirs = call(enter_kernel, [((NS, HALF), F32)] * 2, [VMEM] * 3, "state_in")(
        prefix, keep, got
    )
    got_state = swap(theirs, 1)
    gated, square = call(mix_kernel, [((TOK, COLS), F32), ((8, TOK), F32)], [VMEM] * 6, "mix")(
        y_part, enter, c_in, z_in, mine, got_state
    )
    squares = [square] + [
        lax.ppermute(square, "head", [(i, i ^ bit) for i in range(4)]) for bit in (1, 2, 3)
    ]

    ssm_out, rng = call(
        finish_kernel, [((TOK, COLS), BF16), ((32, 128), BF16)], [VMEM] * 7, "finish",
        scratch=[pltpu.VMEM((32, 128), F32)],
    )(gated, *squares, gain_row, attn_rng)
    (rng,) = call(least_kernel, [((CHIPS, 32, 128), BF16)], [VMEM] * 2, "least")(rng, swap(rng, 1))
    rng = lax.all_to_all(rng, "seq", 0, 0, tiled=True, axis_index_groups=same_core)
    attn_range, ssm_range = call(
        range_kernel, [((2, GROUP * HD), F32), ((2, COLS), F32)], [VMEM], "ranges"
    )(rng)
    return (attn_out, ssm_out, attn_range, ssm_range)


def solution(mesh):
    return jax.shard_map(
        body,
        mesh=mesh,
        in_specs=(
            P("seq", "head"),
            P("seq", "head"),
            P("seq", "head"),
            P("seq", "head"),
            P("seq", "head"),
            P("seq", None),
            P("seq", None),
            P("seq", "head"),
            P("head"),
            P("head"),
            P("head"),
            P("seq"),
        ),
        out_specs=(P("seq", "head"), P("seq", "head"), P(None, "head"), P(None, "head")),
        check_vma=False,
    )
```

```python
import functools
import math

import jax
import jax.numpy as jnp
from jax import lax
from jax.experimental import pallas as pl
from jax.experimental.pallas import tpu as pltpu
from jax.sharding import PartitionSpec as P

TOK = 128
GROUP = 5
HD = 128
HEADS = 16
HP = 64
NS = 256
COLS = 1024
HALF = 512
HALF_HEADS = 8
ALL_COLS = 4096
CHIPS = 32
EPSILON = 1e-05
FLOOR = -1e30
SCORE_SCALE = math.log2(math.e) / math.sqrt(HD)
F32 = jnp.float32
BF16 = jnp.bfloat16
HIGH = lax.Precision.HIGHEST

VMEM = pl.BlockSpec(memory_space=pltpu.VMEM)
SMEM = pl.BlockSpec(memory_space=pltpu.SMEM)
ANY = pl.BlockSpec(memory_space=pl.ANY)


def mm(a, b, dims=((1,), (0,)), precision=None):
    return lax.dot_general(a, b, (dims, ((), ())), precision=precision, preferred_element_type=F32)


def split_mm(a, b, dims=((1,), (0,)), which=0):
    wide = (a, b)[which]
    top = wide.astype(BF16)
    rest = (wide - top.astype(F32)).astype(BF16)
    if which == 0:
        return mm(top, b, dims) + mm(rest, b, dims)
    return mm(a, top, dims) + mm(a, rest, dims)


def iota(shape, dim):
    return lax.broadcasted_iota(jnp.int32, shape, dim)


def spread_heads(first_head, width):
    return jnp.where(
        iota((HEADS, width), 0) == first_head + iota((HEADS, width), 1) // HP, 1.0, 0.0
    ).astype(F32)


def step_sizes(dt_ref, a_ref):
    raw = dt_ref[...]
    step_t = jnp.maximum(raw, 0.0) + jnp.log1p(jnp.exp(-jnp.abs(raw)))
    rows, cols = iota((TOK, TOK), 0), iota((TOK, TOK), 1)
    eye = jnp.where(rows == cols, 1.0, 0.0).astype(F32)
    rate = jnp.exp(jnp.transpose(jnp.broadcast_to(a_ref[...], (TOK, HEADS))))
    upper = jnp.where(rows <= cols, 1.0, 0.0).astype(F32)
    running_t = mm(-step_t * rate, upper, precision=HIGH)
    both = mm(eye, jnp.concatenate([step_t, running_t], axis=0), ((1,), (1,)), precision=HIGH)
    return step_t, running_t, both[:, :HEADS], both[:, HEADS : 2 * HEADS]


def position(doc_smem):
    return lax.axis_index("seq"), doc_smem[0, 0], doc_smem[0, TOK - 1]


def local_kernel(scal, x_ref, b_ref, dt_ref, a_ref, keep_ref, send_ref):
    me, _, last_doc = position(scal)
    begin = me * TOK
    core = me % 2
    _, _, step_len, running = step_sizes(dt_ref, a_ref)
    last = running[TOK - 1 : TOK, :]
    live = begin + iota((TOK, HEADS), 0) >= last_doc
    reach = jnp.where(live, jnp.exp(last - running) * step_len, 0.0)
    through = jnp.where(last_doc < begin, jnp.exp(last), 0.0)
    stacked = jnp.concatenate([reach, jnp.broadcast_to(through, (8, HEADS))], axis=0)
    for half, out in ((core, keep_ref), (1 - core, send_ref)):
        wide = mm(stacked, spread_heads(half * HALF_HEADS, HALF), precision=HIGH)
        values = x_ref[:, pl.ds(pl.multiple_of(half * HALF, HALF), HALF)].astype(F32)
        out[0:NS, :] = split_mm(b_ref[...], values * wide[:TOK], ((0,), (0,)), which=1)
        out[NS : NS + 8, :] = wide[TOK:]


def intra_kernel(x_ref, b_ref, c_ref, dt_ref, a_ref, skip_ref, doc_ref, y_ref, enter_ref):
    begin = lax.axis_index("seq") * TOK
    step_t, running_t, _, running = step_sizes(dt_ref, a_ref)
    rows, cols = iota((TOK, TOK), 0), iota((TOK, TOK), 1)
    doc = jnp.transpose(jnp.broadcast_to(doc_ref[...], (TOK, TOK)).astype(F32)).astype(jnp.int32)
    same_doc = (cols <= rows) & (begin + cols >= doc)
    earlier = same_doc & (cols < rows)
    enter_ref[...] = jnp.where(doc[:, :HEADS] < begin, jnp.exp(running), 0.0)
    inner = jnp.where(same_doc, mm(c_ref[...], b_ref[...], ((1,), (1,))), 0.0)
    skip = mm(
        jnp.broadcast_to(skip_ref[...], (8, HEADS)), spread_heads(0, COLS), precision=HIGH
    )[0:1]
    left = iota((TOK, 2 * HP), 1) < HP
    for pair in range(HEADS // 2):
        parts = []
        for h in (2 * pair, 2 * pair + 1):
            gap = jnp.where(earlier, running[:, h : h + 1] - running_t[h : h + 1, :], 0.0)
            parts.append(inner * jnp.exp(gap) * step_t[h : h + 1, :])
        at = slice(pair * 2 * HP, (pair + 1) * 2 * HP)
        values = x_ref[:, at]
        both = split_mm(jnp.concatenate(parts, axis=0), values)
        y_ref[:, at] = jnp.where(left, both[:TOK], both[TOK:]) + skip[:, at] * values.astype(F32)


def chip_kernel(keep_ref, got_ref, out_ref):
    core = lax.axis_index("seq") % 2
    first = core == 0
    t_own, t_other = keep_ref[NS : NS + 1, :], got_ref[NS : NS + 1, :]
    f_own = jnp.where(first, t_other, 1.0)
    f_other = jnp.where(first, 1.0, t_own)
    through = t_own * t_other
    lines = [through[:, tile * 128 : tile * 128 + 128] for tile in range(4)]
    lines = jnp.concatenate(lines + [jnp.zeros((4, 128), F32)], axis=0)
    for chip in range(CHIPS):
        rows = slice(chip * 8, chip * 8 + 8)
        out_ref[chip, :, 0:HALF] = keep_ref[rows, :] * f_own + got_ref[rows, :] * f_other
        out_ref[chip, :, HALF : HALF + 128] = lines


def prefix_kernel(in_ref, out_ref):
    total = jnp.zeros((8, HALF), F32)
    for chip in range(CHIPS):
        out_ref[chip] = total
        if chip < CHIPS - 1:
            lines = in_ref[chip, :, HALF : HALF + 128]
            through = jnp.concatenate([lines[n : n + 1] for n in range(4)], axis=1)
            total = total * through + in_ref[chip, :, 0:HALF]


def enter_kernel(pre_ref, keep_ref, got_ref, mine_ref, send_ref):
    core = lax.axis_index("seq") % 2
    first = core == 0
    t_first = jnp.where(first, keep_ref[NS : NS + 1, :], got_ref[NS : NS + 1, :])
    for chip in range(CHIPS):
        rows = slice(chip * 8, chip * 8 + 8)
        before = pre_ref[chip]
        state = jnp.where(first, keep_ref[rows, :], got_ref[rows, :])
        after = before * t_first + state
        mine_ref[rows, :] = jnp.where(first, before, after)
        send_ref[rows, :] = jnp.where(first, after, before)


def mix_kernel(y_ref, enter_ref, c_ref, z_ref, mine_ref, got_ref, gated_ref, sq_ref):
    core = lax.axis_index("seq") % 2
    squares = jnp.zeros((TOK, 128), F32)
    for half, state in ((core, mine_ref), (1 - core, got_ref)):
        at = pl.ds(pl.multiple_of(half * HALF, HALF), HALF)
        wide = mm(enter_ref[...], spread_heads(half * HALF_HEADS, HALF), precision=HIGH)
        mixed = y_ref[:, at] + split_mm(c_ref[...], state[...], which=1) * wide
        gate = z_ref[:, at].astype(F32)
        gated = mixed * (gate / (1.0 + jnp.exp(-gate)))
        gated_ref[:, at] = gated
        power = gated * gated
        for tile in range(HALF // 128):
            squares += power[:, tile * 128 : tile * 128 + 128]
    ones = jnp.ones((8, 128), F32)
    sq_ref[...] = mm(ones, squares, ((1,), (1,)), precision=HIGH)


def finish_kernel(gated_ref, s0, s1, s2, s3, gain_ref, attn_rng, out_ref, rng_ref, lines):
    total = s0[...] + s1[...] + s2[...] + s3[...]
    scale = lax.rsqrt(total[0:1, :] / ALL_COLS + EPSILON)
    scale = jnp.transpose(jnp.broadcast_to(scale, (TOK, TOK)))
    lines[16:32, :] = attn_rng[...]
    for tile in range(COLS // 128):
        at = slice(tile * 128, tile * 128 + 128)
        out = (gated_ref[:, at] * scale * gain_ref[:, at]).astype(BF16)
        out_ref[:, at] = out
        wide = out.astype(F32)
        lines[tile : tile + 1, :] = jnp.min(wide, axis=0, keepdims=True)
        lines[8 + tile : 9 + tile, :] = jnp.min(-wide, axis=0, keepdims=True)
    rng_ref[...] = lines[...].astype(BF16)


def least_kernel(own_ref, got_ref, out_ref):
    least = jnp.minimum(own_ref[...].astype(F32), got_ref[...].astype(F32)).astype(BF16)
    for dest in range(CHIPS):
        out_ref[dest] = least


def range_kernel(in_ref, attn_ref, ssm_ref):
    least = in_ref[0].astype(F32)
    for part in range(1, CHIPS):
        least = jnp.minimum(least, in_ref[part].astype(F32))
    for tile in range(COLS // 128):
        at = slice(tile * 128, tile * 128 + 128)
        ssm_ref[0:1, at] = least[tile : tile + 1]
        ssm_ref[1:2, at] = -least[8 + tile : 9 + tile]
    for tile in range(GROUP):
        at = slice(tile * 128, tile * 128 + 128)
        attn_ref[0:1, at] = least[16 + tile : 17 + tile]
        attn_ref[1:2, at] = -least[21 + tile : 22 + tile]


ROWS = GROUP * TOK


def attn_kernel(flips, span, first, final, doc_smem, q_ref, doc_ref, *rest):
    sides, rest = rest[: 4 * len(flips)], rest[4 * len(flips) :]
    if not first:
        (old_highest, old_totals, old_accum), rest = [rest[0].at[n] for n in range(3)], rest[1:]
    if final:
        out_ref, rng_ref, carry, q_rows = rest
    else:
        carry, q_rows = rest
    highest, totals, accum = [carry.at[n] for n in range(3)]
    me, first_doc, last_doc = position(doc_smem)
    core, z_mine, x_mine = me % 2, me // 8, me // 2 % 4
    wide = span * TOK
    width = 2 * len(flips) * wide
    lane = iota((TOK, wide), 1)
    lane = lane // TOK * (8 * TOK) + lane % TOK
    for g in range(GROUP):
        q_rows[g * TOK : (g + 1) * TOK, :] = q_ref[:, g * HD : (g + 1) * HD]

    def load(planes, which):
        refs = [sides[2 * n + which] for n in range(2 * len(flips))]
        at = [slice(0, HD) if ref.shape[2] == HD or which == 0 else slice(HD, 2 * HD) for ref in refs]
        return jnp.concatenate(
            [ref[planes, :, cols].reshape(wide, HD) for ref, cols in zip(refs, at)], axis=0
        )

    def hide(block, values):
        begins = [
            ((block * span * 4 + (x_mine ^ flip)) * 2 + side) * TOK
            for flip in flips
            for side in (core, 1 - core)
        ]
        key_pos = jnp.concatenate([begin + lane for begin in begins], axis=1)
        doc = jnp.transpose(jnp.broadcast_to(doc_ref[...], (TOK, TOK)).astype(F32))
        doc = jnp.concatenate([doc.astype(jnp.int32)] * (width // TOK), axis=1)
        q_pos = me * TOK + iota((TOK, width), 0)
        visible = (key_pos <= q_pos) & (key_pos >= doc)
        return jnp.where(jnp.concatenate([visible] * GROUP, axis=0), values, FLOOR)

    def score(block, masked):
        keys = load(pl.ds(block * span, span), 0)
        scores = mm(q_rows[...], keys, ((1,), (1,)))
        return hide(block, scores) if masked else scores

    def fold(join, values):
        total = values[:, :TOK]
        for n in range(1, width // TOK):
            total = join(total, values[:, n * TOK : (n + 1) * TOK])
        return total

    def absorb(block, masked):
        vals = load(pl.ds(block * span, span), 1)
        scores = score(block, masked)
        old = highest[...]
        new = jnp.maximum(old, jnp.max(fold(jnp.maximum, scores), axis=1, keepdims=True))
        factor = jnp.exp2((old - new) * SCORE_SCALE)
        gap = scores - jnp.concatenate([new] * (width // TOK), axis=1)
        weights = jnp.exp2(gap * SCORE_SCALE)
        highest[...] = new
        totals[...] = totals[...] * factor + fold(jnp.add, weights)
        accum[...] = accum[...] * factor + mm(weights.astype(BF16), vals)

    size = span * 8 * TOK
    low, last = first_doc // size, z_mine // span
    inner = jnp.minimum((last_doc + size - 1) // size, last)

    def edge(n, _):
        absorb(jnp.where(n == 0, last, low + n - 1), True)
        return 0

    def inside(block, _):
        absorb(block, False)
        return 0

    if first:
        highest[...] = jnp.full((ROWS, HD), 0.1 * FLOOR, F32)
        totals[...] = jnp.zeros((ROWS, HD), F32)
        accum[...] = jnp.zeros((ROWS, HD), F32)
    else:
        highest[...] = old_highest[...]
        totals[...] = old_totals[...]
        accum[...] = old_accum[...]
    lax.fori_loop(0, inner - low + 1, edge, 0)
    lax.fori_loop(inner, last, inside, 0)
    if not final:
        return
    rng_ref[...] = jnp.zeros(rng_ref.shape, F32)
    for g in range(GROUP):
        rows = slice(g * TOK, (g + 1) * TOK)
        total = jnp.sum(totals[rows, :], axis=1, keepdims=True)
        out = (accum[rows, :] / total).astype(BF16)
        out_ref[:, g * HD : (g + 1) * HD] = out
        values = out.astype(F32)
        rng_ref[g : g + 1, :] = jnp.min(values, axis=0, keepdims=True)
        rng_ref[GROUP + g : GROUP + g + 1, :] = jnp.min(-values, axis=0, keepdims=True)


ATTN_COST = 10**10


def call(kernel, outs, specs, name, scratch=(), flops=0):
    return pl.pallas_call(
        kernel,
        out_shape=[jax.ShapeDtypeStruct(shape, dtype) for shape, dtype in outs],
        in_specs=list(specs),
        out_specs=[VMEM] * len(outs),
        scratch_shapes=list(scratch),
        compiler_params=pltpu.CompilerParams(vmem_limit_bytes=40 * 2**20),
        cost_estimate=pl.CostEstimate(flops=flops, bytes_accessed=0, transcendentals=0),
        name=name,
    )


def swap(value, bit):
    count = lax.axis_size("seq")
    return lax.ppermute(value, "seq", [(i, i ^ bit) for i in range(count)])


def body(q_in, k_in, v_in, x_in, z_in, b_in, c_in, dt_raw, a_log, d_skip, ssm_gain, doc_start):
    dt_t = dt_raw.T
    doc_row = doc_start[None, :]
    a_row, skip_row, gain_row = a_log[None, :], d_skip[None, :], ssm_gain[None, :]
    same_core = [[i for i in range(64) if i % 2 == core] for core in range(2)]
    column = [[z * 8 + n for z in range(8)] for n in range(8)]

    near = jnp.concatenate([k_in, v_in], axis=1)[None]
    near = jnp.broadcast_to(near, (8, TOK, 2 * HD))
    near = lax.all_to_all(near, "seq", 0, 0, tiled=True, axis_index_groups=column)

    def attend(parts, flips, span, first, final, carry, name):
        scratch = [pltpu.VMEM((ROWS, HD), BF16)]
        if final:
            outs = [((TOK, GROUP * HD), BF16), ((16, 128), F32)]
            scratch = [pltpu.VMEM((3, ROWS, HD), F32)] + scratch
        else:
            outs = [((3, ROWS, HD), F32)]
        refs = []
        for part in parts:
            other = [swap(value, 1) for value in part]
            refs += [part[0], part[-1], other[0], other[-1]]
        return call(
            functools.partial(attn_kernel, flips, span, first, final), outs,
            [SMEM] + [VMEM] * (2 + len(refs) + len(carry)), name, scratch=scratch, flops=9*10**9 if first else ATTN_COST,
        )(doc_row, q_in, doc_row, *refs, *carry)

    keep, send = call(
        local_kernel, [((NS + 8, HALF), F32)] * 2, [SMEM] + [VMEM] * 4, "local_state"
    )(doc_row, x_in, b_in, dt_t, a_row)
    got = swap(send, 1)
    y_part, enter = call(
        intra_kernel, [((TOK, COLS), F32), ((TOK, HEADS), F32)], [VMEM] * 7, "intra"
    )(x_in, b_in, c_in, dt_t, a_row, skip_row, doc_row)
    (chunks,) = call(chip_kernel, [((CHIPS, 8, HALF + 128), F32)], [VMEM] * 2, "chip_state")(keep, got)
    near, chunks, y_part = lax.optimization_barrier((near, chunks, y_part))
    chunks = lax.all_to_all(chunks, "seq", 0, 0, tiled=True, axis_index_groups=same_core)
    side1, side3 = swap(near, 2), swap(near, 6)
    carry = attend([[near]], (0,), 4, True, False, [], "attention_near")
    far = [swap(side1[:, :, :HD], 6), swap(side3[:, :, HD:], 2)]
    chunks, _, _ = lax.optimization_barrier((chunks, carry, far))
    carry = attend([[side1], [side3]], (1, 3), 2, False, False, carry, "attention_sides")
    (prefix,) = call(prefix_kernel, [((CHIPS, 8, HALF), F32)], [VMEM], "prefix")(chunks)
    prefix = lax.all_to_all(prefix, "seq", 0, 0, tiled=True, axis_index_groups=same_core)
    attn_out, attn_rng = attend([far], (2,), 4, False, True, carry, "attention_far")
    prefix, attn_rng = lax.optimization_barrier((prefix, attn_rng))
    mine, theirs = call(enter_kernel, [((NS, HALF), F32)] * 2, [VMEM] * 3, "state_in")(
        prefix, keep, got
    )
    got_state = swap(theirs, 1)
    gated, square = call(mix_kernel, [((TOK, COLS), F32), ((8, TOK), F32)], [VMEM] * 6, "mix")(
        y_part, enter, c_in, z_in, mine, got_state
    )
    squares = [square] + [
        lax.ppermute(square, "head", [(i, i ^ bit) for i in range(4)]) for bit in (1, 2, 3)
    ]

    ssm_out, rng = call(
        finish_kernel, [((TOK, COLS), BF16), ((32, 128), BF16)], [VMEM] * 7, "finish",
        scratch=[pltpu.VMEM((32, 128), F32)],
    )(gated, *squares, gain_row, attn_rng)
    (rng,) = call(least_kernel, [((CHIPS, 32, 128), BF16)], [VMEM] * 2, "least")(rng, swap(rng, 1))
    rng = lax.all_to_all(rng, "seq", 0, 0, tiled=True, axis_index_groups=same_core)
    attn_range, ssm_range = call(
        range_kernel, [((2, GROUP * HD), F32), ((2, COLS), F32)], [VMEM], "ranges"
    )(rng)
    return (attn_out, ssm_out, attn_range, ssm_range)


def solution(mesh):
    return jax.shard_map(
        body,
        mesh=mesh,
        in_specs=(
            P("seq", "head"),
            P("seq", "head"),
            P("seq", "head"),
            P("seq", "head"),
            P("seq", "head"),
            P("seq", None),
            P("seq", None),
            P("seq", "head"),
            P("head"),
            P("head"),
            P("head"),
            P("seq"),
        ),
        out_specs=(P("seq", "head"), P("seq", "head"), P(None, "head"), P(None, "head")),
        check_vma=False,
    )
```

```python
import functools
import math

import jax
import jax.numpy as jnp
from jax import lax
from jax.experimental import pallas as pl
from jax.experimental.pallas import tpu as pltpu
from jax.sharding import PartitionSpec as P

TOK = 128
GROUP = 5
HD = 128
HEADS = 16
HP = 64
NS = 256
COLS = 1024
HALF = 512
HALF_HEADS = 8
ALL_COLS = 4096
CHIPS = 32
EPSILON = 1e-05
FLOOR = -1e30
SCORE_SCALE = math.log2(math.e) / math.sqrt(HD)
F32 = jnp.float32
BF16 = jnp.bfloat16
HIGH = lax.Precision.HIGHEST

VMEM = pl.BlockSpec(memory_space=pltpu.VMEM)
SMEM = pl.BlockSpec(memory_space=pltpu.SMEM)
ANY = pl.BlockSpec(memory_space=pl.ANY)


def mm(a, b, dims=((1,), (0,)), precision=None):
    return lax.dot_general(a, b, (dims, ((), ())), precision=precision, preferred_element_type=F32)


def split_mm(a, b, dims=((1,), (0,)), which=0):
    wide = (a, b)[which]
    top = wide.astype(BF16)
    rest = (wide - top.astype(F32)).astype(BF16)
    if which == 0:
        return mm(top, b, dims) + mm(rest, b, dims)
    return mm(a, top, dims) + mm(a, rest, dims)


def iota(shape, dim):
    return lax.broadcasted_iota(jnp.int32, shape, dim)


def spread_heads(first_head, width):
    return jnp.where(
        iota((HEADS, width), 0) == first_head + iota((HEADS, width), 1) // HP, 1.0, 0.0
    ).astype(F32)


def step_sizes(dt_ref, a_ref):
    raw = dt_ref[...]
    step_t = jnp.maximum(raw, 0.0) + jnp.log1p(jnp.exp(-jnp.abs(raw)))
    rows, cols = iota((TOK, TOK), 0), iota((TOK, TOK), 1)
    eye = jnp.where(rows == cols, 1.0, 0.0).astype(F32)
    rate = jnp.exp(jnp.transpose(jnp.broadcast_to(a_ref[...], (TOK, HEADS))))
    upper = jnp.where(rows <= cols, 1.0, 0.0).astype(F32)
    running_t = mm(-step_t * rate, upper, precision=HIGH)
    both = mm(eye, jnp.concatenate([step_t, running_t], axis=0), ((1,), (1,)), precision=HIGH)
    return step_t, running_t, both[:, :HEADS], both[:, HEADS : 2 * HEADS]


def position(doc_smem):
    return lax.axis_index("seq"), doc_smem[0, 0], doc_smem[0, TOK - 1]


def local_kernel(scal, x_ref, b_ref, dt_ref, a_ref, keep_ref, send_ref):
    me, _, last_doc = position(scal)
    begin = me * TOK
    core = me % 2
    _, _, step_len, running = step_sizes(dt_ref, a_ref)
    last = running[TOK - 1 : TOK, :]
    live = begin + iota((TOK, HEADS), 0) >= last_doc
    reach = jnp.where(live, jnp.exp(last - running) * step_len, 0.0)
    through = jnp.where(last_doc < begin, jnp.exp(last), 0.0)
    stacked = jnp.concatenate([reach, jnp.broadcast_to(through, (8, HEADS))], axis=0)
    for half, out in ((core, keep_ref), (1 - core, send_ref)):
        wide = mm(stacked, spread_heads(half * HALF_HEADS, HALF), precision=HIGH)
        values = x_ref[:, pl.ds(pl.multiple_of(half * HALF, HALF), HALF)].astype(F32)
        out[0:NS, :] = split_mm(b_ref[...], values * wide[:TOK], ((0,), (0,)), which=1)
        out[NS : NS + 8, :] = wide[TOK:]


def intra_kernel(x_ref, b_ref, c_ref, dt_ref, a_ref, skip_ref, doc_ref, z_ref, y_ref, enter_ref, gate_ref):
    begin = lax.axis_index("seq") * TOK
    step_t, running_t, _, running = step_sizes(dt_ref, a_ref)
    rows, cols = iota((TOK, TOK), 0), iota((TOK, TOK), 1)
    doc = jnp.transpose(jnp.broadcast_to(doc_ref[...], (TOK, TOK)).astype(F32)).astype(jnp.int32)
    same_doc = (cols <= rows) & (begin + cols >= doc)
    earlier = same_doc & (cols < rows)
    enter = jnp.where(doc[:, :HEADS] < begin, jnp.exp(running), 0.0)
    enter_ref[...] = mm(enter, spread_heads(0, COLS), precision=HIGH)
    gate = z_ref[...].astype(F32)
    gate_ref[...] = gate / (1.0 + jnp.exp(-gate))
    inner = jnp.where(same_doc, mm(c_ref[...], b_ref[...], ((1,), (1,))), 0.0)
    skip = mm(
        jnp.broadcast_to(skip_ref[...], (8, HEADS)), spread_heads(0, COLS), precision=HIGH
    )[0:1]
    left = iota((TOK, 2 * HP), 1) < HP
    for pair in range(HEADS // 2):
        parts = []
        for h in (2 * pair, 2 * pair + 1):
            gap = jnp.where(earlier, running[:, h : h + 1] - running_t[h : h + 1, :], 0.0)
            parts.append(inner * jnp.exp(gap) * step_t[h : h + 1, :])
        at = slice(pair * 2 * HP, (pair + 1) * 2 * HP)
        values = x_ref[:, at]
        both = split_mm(jnp.concatenate(parts, axis=0), values)
        y_ref[:, at] = jnp.where(left, both[:TOK], both[TOK:]) + skip[:, at] * values.astype(F32)


def chip_kernel(keep_ref, got_ref, out_ref):
    core = lax.axis_index("seq") % 2
    first = core == 0
    t_own, t_other = keep_ref[NS : NS + 1, :], got_ref[NS : NS + 1, :]
    f_own = jnp.where(first, t_other, 1.0)
    f_other = jnp.where(first, 1.0, t_own)
    through = t_own * t_other
    lines = [through[:, tile * 128 : tile * 128 + 128] for tile in range(4)]
    lines = jnp.concatenate(lines + [jnp.zeros((4, 128), F32)], axis=0)
    for chip in range(CHIPS):
        rows = slice(chip * 8, chip * 8 + 8)
        out_ref[chip, :, 0:HALF] = keep_ref[rows, :] * f_own + got_ref[rows, :] * f_other
        out_ref[chip, :, HALF : HALF + 128] = lines


def prefix_kernel(in_ref, out_ref):
    total = jnp.zeros((8, HALF), F32)
    for chip in range(CHIPS):
        out_ref[chip] = total
        if chip < CHIPS - 1:
            lines = in_ref[chip, :, HALF : HALF + 128]
            through = jnp.concatenate([lines[n : n + 1] for n in range(4)], axis=1)
            total = total * through + in_ref[chip, :, 0:HALF]


def enter_kernel(pre_ref, keep_ref, got_ref, mine_ref, send_ref):
    core = lax.axis_index("seq") % 2
    first = core == 0
    t_first = jnp.where(first, keep_ref[NS : NS + 1, :], got_ref[NS : NS + 1, :])
    for chip in range(CHIPS):
        rows = slice(chip * 8, chip * 8 + 8)
        before = pre_ref[chip]
        state = jnp.where(first, keep_ref[rows, :], got_ref[rows, :])
        after = before * t_first + state
        mine_ref[rows, :] = jnp.where(first, before, after)
        send_ref[rows, :] = jnp.where(first, after, before)


def mix_kernel(y_ref, enter_ref, c_ref, gate_ref, mine_ref, got_ref, gated_ref, sq_ref):
    core = lax.axis_index("seq") % 2
    squares = jnp.zeros((TOK, 128), F32)
    for half, state in ((core, mine_ref), (1 - core, got_ref)):
        at = pl.ds(pl.multiple_of(half * HALF, HALF), HALF)
        mixed = y_ref[:, at] + split_mm(c_ref[...], state[...], which=1) * enter_ref[:, at]
        gated = mixed * gate_ref[:, at]
        gated_ref[:, at] = gated
        power = gated * gated
        for tile in range(HALF // 128):
            squares += power[:, tile * 128 : tile * 128 + 128]
    ones = jnp.ones((8, 128), F32)
    sq_ref[...] = mm(ones, squares, ((1,), (1,)), precision=HIGH)


def finish_kernel(gated_ref, s0, s1, s2, s3, gain_ref, attn_rng, out_ref, rng_ref, lines):
    total = s0[...] + s1[...] + s2[...] + s3[...]
    scale = lax.rsqrt(total[0:1, :] / ALL_COLS + EPSILON)
    scale = jnp.transpose(jnp.broadcast_to(scale, (TOK, TOK)))
    lines[16:32, :] = attn_rng[...]
    for tile in range(COLS // 128):
        at = slice(tile * 128, tile * 128 + 128)
        out = (gated_ref[:, at] * scale * gain_ref[:, at]).astype(BF16)
        out_ref[:, at] = out
        wide = out.astype(F32)
        lines[tile : tile + 1, :] = jnp.min(wide, axis=0, keepdims=True)
        lines[8 + tile : 9 + tile, :] = jnp.min(-wide, axis=0, keepdims=True)
    rng_ref[...] = lines[...].astype(BF16)


def least_kernel(own_ref, got_ref, out_ref):
    least = jnp.minimum(own_ref[...].astype(F32), got_ref[...].astype(F32)).astype(BF16)
    for dest in range(CHIPS):
        out_ref[dest] = least


def range_kernel(in_ref, attn_ref, ssm_ref):
    least = in_ref[0].astype(F32)
    for part in range(1, CHIPS):
        least = jnp.minimum(least, in_ref[part].astype(F32))
    for tile in range(COLS // 128):
        at = slice(tile * 128, tile * 128 + 128)
        ssm_ref[0:1, at] = least[tile : tile + 1]
        ssm_ref[1:2, at] = -least[8 + tile : 9 + tile]
    for tile in range(GROUP):
        at = slice(tile * 128, tile * 128 + 128)
        attn_ref[0:1, at] = least[16 + tile : 17 + tile]
        attn_ref[1:2, at] = -least[21 + tile : 22 + tile]


ROWS = GROUP * TOK


def attn_kernel(flips, span, first, final, doc_smem, q_ref, doc_ref, *rest):
    sides, rest = rest[: 4 * len(flips)], rest[4 * len(flips) :]
    if not first:
        (old_highest, old_totals, old_accum), rest = [rest[0].at[n] for n in range(3)], rest[1:]
    if final:
        out_ref, rng_ref, carry, q_rows = rest
    else:
        carry, q_rows = rest
    highest, totals, accum = [carry.at[n] for n in range(3)]
    me, first_doc, last_doc = position(doc_smem)
    core, z_mine, x_mine = me % 2, me // 8, me // 2 % 4
    wide = span * TOK
    width = 2 * len(flips) * wide
    lane = iota((TOK, wide), 1)
    lane = lane // TOK * (8 * TOK) + lane % TOK
    for g in range(GROUP):
        q_rows[g * TOK : (g + 1) * TOK, :] = q_ref[:, g * HD : (g + 1) * HD]

    def load(planes, which):
        refs = [sides[2 * n + which] for n in range(2 * len(flips))]
        at = [slice(0, HD) if ref.shape[2] == HD or which == 0 else slice(HD, 2 * HD) for ref in refs]
        return jnp.concatenate(
            [ref[planes, :, cols].reshape(wide, HD) for ref, cols in zip(refs, at)], axis=0
        )

    def hide(block, values):
        begins = [
            ((block * span * 4 + (x_mine ^ flip)) * 2 + side) * TOK
            for flip in flips
            for side in (core, 1 - core)
        ]
        key_pos = jnp.concatenate([begin + lane for begin in begins], axis=1)
        doc = jnp.transpose(jnp.broadcast_to(doc_ref[...], (TOK, TOK)).astype(F32))
        doc = jnp.concatenate([doc.astype(jnp.int32)] * (width // TOK), axis=1)
        q_pos = me * TOK + iota((TOK, width), 0)
        visible = (key_pos <= q_pos) & (key_pos >= doc)
        return jnp.where(jnp.concatenate([visible] * GROUP, axis=0), values, FLOOR)

    def score(block, masked):
        keys = load(pl.ds(block * span, span), 0)
        scores = mm(q_rows[...], keys, ((1,), (1,)))
        return hide(block, scores) if masked else scores

    def fold(join, values):
        total = values[:, :TOK]
        for n in range(1, width // TOK):
            total = join(total, values[:, n * TOK : (n + 1) * TOK])
        return total

    def absorb(block, masked):
        vals = load(pl.ds(block * span, span), 1)
        scores = score(block, masked)
        old = highest[...]
        new = jnp.maximum(old, jnp.max(fold(jnp.maximum, scores), axis=1, keepdims=True))
        factor = jnp.exp2((old - new) * SCORE_SCALE)
        gap = scores - jnp.concatenate([new] * (width // TOK), axis=1)
        weights = jnp.exp2(gap * SCORE_SCALE)
        highest[...] = new
        totals[...] = totals[...] * factor + fold(jnp.add, weights)
        accum[...] = accum[...] * factor + mm(weights.astype(BF16), vals)

    size = span * 8 * TOK
    low, last = first_doc // size, z_mine // span
    inner = jnp.minimum((last_doc + size - 1) // size, last)

    def edge(n, _):
        absorb(jnp.where(n == 0, last, low + n - 1), True)
        return 0

    def inside(block, _):
        absorb(block, False)
        return 0

    if first:
        highest[...] = jnp.full((ROWS, HD), 0.1 * FLOOR, F32)
        totals[...] = jnp.zeros((ROWS, HD), F32)
        accum[...] = jnp.zeros((ROWS, HD), F32)
    else:
        highest[...] = old_highest[...]
        totals[...] = old_totals[...]
        accum[...] = old_accum[...]
    lax.fori_loop(0, inner - low + 1, edge, 0)
    lax.fori_loop(inner, last, inside, 0)
    if not final:
        return
    rng_ref[...] = jnp.zeros(rng_ref.shape, F32)
    for g in range(GROUP):
        rows = slice(g * TOK, (g + 1) * TOK)
        total = jnp.sum(totals[rows, :], axis=1, keepdims=True)
        out = (accum[rows, :] / total).astype(BF16)
        out_ref[:, g * HD : (g + 1) * HD] = out
        values = out.astype(F32)
        rng_ref[g : g + 1, :] = jnp.min(values, axis=0, keepdims=True)
        rng_ref[GROUP + g : GROUP + g + 1, :] = jnp.min(-values, axis=0, keepdims=True)


ATTN_COST = 10**10


def call(kernel, outs, specs, name, scratch=(), flops=0):
    return pl.pallas_call(
        kernel,
        out_shape=[jax.ShapeDtypeStruct(shape, dtype) for shape, dtype in outs],
        in_specs=list(specs),
        out_specs=[VMEM] * len(outs),
        scratch_shapes=list(scratch),
        compiler_params=pltpu.CompilerParams(vmem_limit_bytes=40 * 2**20),
        cost_estimate=pl.CostEstimate(flops=flops, bytes_accessed=0, transcendentals=0),
        name=name,
    )


def swap(value, bit):
    count = lax.axis_size("seq")
    return lax.ppermute(value, "seq", [(i, i ^ bit) for i in range(count)])


def body(q_in, k_in, v_in, x_in, z_in, b_in, c_in, dt_raw, a_log, d_skip, ssm_gain, doc_start):
    dt_t = dt_raw.T
    doc_row = doc_start[None, :]
    a_row, skip_row, gain_row = a_log[None, :], d_skip[None, :], ssm_gain[None, :]
    same_core = [[i for i in range(64) if i % 2 == core] for core in range(2)]
    column = [[z * 8 + n for z in range(8)] for n in range(8)]

    near = jnp.concatenate([k_in, v_in], axis=1)[None]
    near = jnp.broadcast_to(near, (8, TOK, 2 * HD))
    near = lax.all_to_all(near, "seq", 0, 0, tiled=True, axis_index_groups=column)

    def attend(parts, flips, span, first, final, carry, name):
        scratch = [pltpu.VMEM((ROWS, HD), BF16)]
        if final:
            outs = [((TOK, GROUP * HD), BF16), ((16, 128), F32)]
            scratch = [pltpu.VMEM((3, ROWS, HD), F32)] + scratch
        else:
            outs = [((3, ROWS, HD), F32)]
        refs = []
        for part in parts:
            other = [swap(value, 1) for value in part]
            refs += [part[0], part[-1], other[0], other[-1]]
        return call(
            functools.partial(attn_kernel, flips, span, first, final), outs,
            [SMEM] + [VMEM] * (2 + len(refs) + len(carry)), name, scratch=scratch, flops=9*10**9 if first else ATTN_COST,
        )(doc_row, q_in, doc_row, *refs, *carry)

    keep, send = call(
        local_kernel, [((NS + 8, HALF), F32)] * 2, [SMEM] + [VMEM] * 4, "local_state"
    )(doc_row, x_in, b_in, dt_t, a_row)
    got = swap(send, 1)
    y_part, enter, gate = call(
        intra_kernel, [((TOK, COLS), F32)] * 3, [VMEM] * 8, "intra"
    )(x_in, b_in, c_in, dt_t, a_row, skip_row, doc_row, z_in)
    (chunks,) = call(chip_kernel, [((CHIPS, 8, HALF + 128), F32)], [VMEM] * 2, "chip_state")(keep, got)
    near, chunks, y_part = lax.optimization_barrier((near, chunks, y_part))
    chunks = lax.all_to_all(chunks, "seq", 0, 0, tiled=True, axis_index_groups=same_core)
    side1, side3 = swap(near, 2), swap(near, 6)
    carry = attend([[near]], (0,), 4, True, False, [], "attention_near")
    far = [swap(side1[:, :, :HD], 6), swap(side3[:, :, HD:], 2)]
    chunks, _, _ = lax.optimization_barrier((chunks, carry, far))
    carry = attend([[side1], [side3]], (1, 3), 2, False, False, carry, "attention_sides")
    (prefix,) = call(prefix_kernel, [((CHIPS, 8, HALF), F32)], [VMEM], "prefix")(chunks)
    prefix = lax.all_to_all(prefix, "seq", 0, 0, tiled=True, axis_index_groups=same_core)
    attn_out, attn_rng = attend([far], (2,), 4, False, True, carry, "attention_far")
    prefix, attn_rng = lax.optimization_barrier((prefix, attn_rng))
    mine, theirs = call(enter_kernel, [((NS, HALF), F32)] * 2, [VMEM] * 3, "state_in")(
        prefix, keep, got
    )
    got_state = swap(theirs, 1)
    gated, square = call(mix_kernel, [((TOK, COLS), F32), ((8, TOK), F32)], [VMEM] * 6, "mix")(
        y_part, enter, c_in, gate, mine, got_state
    )
    squares = [square] + [
        lax.ppermute(square, "head", [(i, i ^ bit) for i in range(4)]) for bit in (1, 2, 3)
    ]

    ssm_out, rng = call(
        finish_kernel, [((TOK, COLS), BF16), ((32, 128), BF16)], [VMEM] * 7, "finish",
        scratch=[pltpu.VMEM((32, 128), F32)],
    )(gated, *squares, gain_row, attn_rng)
    (rng,) = call(least_kernel, [((CHIPS, 32, 128), BF16)], [VMEM] * 2, "least")(rng, swap(rng, 1))
    rng = lax.all_to_all(rng, "seq", 0, 0, tiled=True, axis_index_groups=same_core)
    attn_range, ssm_range = call(
        range_kernel, [((2, GROUP * HD), F32), ((2, COLS), F32)], [VMEM], "ranges"
    )(rng)
    return (attn_out, ssm_out, attn_range, ssm_range)


def solution(mesh):
    return jax.shard_map(
        body,
        mesh=mesh,
        in_specs=(
            P("seq", "head"),
            P("seq", "head"),
            P("seq", "head"),
            P("seq", "head"),
            P("seq", "head"),
            P("seq", None),
            P("seq", None),
            P("seq", "head"),
            P("head"),
            P("head"),
            P("head"),
            P("seq"),
        ),
        out_specs=(P("seq", "head"), P("seq", "head"), P(None, "head"), P(None, "head")),
        check_vma=False,
    )
```
